32 devices in a mesh: dp: 2 (over x), ctx: 16 (over z, y, core).
Axes of the slice: x: 2, y: 2, z: 4, core: 2. Of those that a mesh axis runs over, the one named last changes fastest.
Arguments:
- fwd_proj: bfloat16 [4096, 3072], P(('dp', 'ctx')), parts along dimension 0, may hold values from -6 to 6
- rev_proj: bfloat16 [4096, 3072], P(('dp', 'ctx')), parts along dimension 0, may hold values from -6 to 6
- tokens: int32 [4096], P(('dp', 'ctx')), parts along dimension 0, may hold values from 0 to 4
- short_taps: float32 [3, 3072], replicated, may hold values from -3.5 to 3.5
- long_kernel: float32 [1024, 2048], P('ctx'), may hold values from -1 to 1
- skip_gain: float32 [1024], P('ctx'), may hold values from -4 to 4
- out_weight: bfloat16 [1024, 1024], replicated, may hold values from -0.1875 to 0.1875
Outputs:
- mixed: bfloat16 [4096, 1024], P(('dp', 'ctx')), parts along dimension 0
The draws below stay inside these ranges and needn't reach their ends.
There are 2 independent parts, one for each index of `dp`. The reference program is written for one: setup_inputs(seed, part) draws one part's arguments, and reference() takes and returns one part's arrays. A program takes and returns all parts, laid end to end along the dimension named above; an argument that names none is the same for every part. Nothing has to cross between parts.
Inputs may be any that keep to these rules, and one draw needn't show every extreme that they name: `tokens`: base of each position, 0 to 3 for A, C, G, T and 4 for an unknown base N.
All inputs are finite; a program needn't handle non-finite values.
Results may differ from the reference program's by a relative error of at most 0.0064.
Values may be sent and summed in bfloat16 or wider, within the bound.
No kernel may reach another device: no remote copies, remote signals or barrier semaphores. Data moves between devices by JAX's collectives and lax.ppermute only.
A program may use at most 64 MiB of HBM per device.

```python
import math
import jax
import jax.numpy as jnp

D = 1024
SEQ = 2048


def draw_long_kernel(key, part):
    key = jax.random.fold_in(key, 7)
    rate_key, base_key = jax.random.split(key)
    rates = jnp.exp(jax.random.uniform(rate_key, (D, 1), jnp.float32, math.log(0.5), math.log(8.0)))
    lags = jnp.arange(SEQ, dtype=jnp.float32)[None, :] / SEQ
    envelope = jnp.exp(-rates * lags)
    base = jnp.clip(jax.random.normal(base_key, (D, SEQ), jnp.float32), -4.0, 4.0)
    return 2.0 * base * envelope / math.sqrt(SEQ)


def with_ends(drawn, stream_key, least, largest):
    longest = drawn.shape.index(max(drawn.shape))
    spots = []
    for shift in (0, 1):
        where = [jax.random.randint(jax.random.fold_in(stream_key, axis), (), 0, length) for axis, length in enumerate(drawn.shape)]
        where[longest] = (where[longest] + shift) % drawn.shape[longest]
        spots.append(tuple(where))
    return drawn.at[spots[0]].set(least).at[spots[1]].set(largest)


def steps_of(rng, extent, pieces, low, high):
    level = 1.0
    for dim, shards_of in pieces:
        heights = jax.random.uniform(jax.random.fold_in(jax.random.fold_in(rng, 6), dim), (shards_of,), jnp.float32, low / len(pieces), high / len(pieces))
        level = level * jnp.repeat(jnp.exp(heights), extent[dim] // shards_of).reshape((-1,) + (1,) * (len(extent) - 1 - dim))
    return level


def bell_draw(own_key, shape, deviation, reach, cuts=(), kind=jnp.bfloat16):
    result = jax.random.normal(own_key, shape, jnp.float32) * deviation
    if len(cuts) > 0:
        result = steps_of(own_key, shape, cuts, -0.22, 0.18) * result
    return jnp.clip(result, min=-reach, max=reach).astype(kind)


def setup_inputs(seed: int = 0, part: int = 0) -> dict:
    key_of = jax.random.split(jax.random.key(seed), 8)
    part_splits = jax.random.split(jax.random.fold_in(key_of[7], part), 8)
    return {
        "fwd_proj": bell_draw(part_splits[0], (SEQ, 3 * D), 1.0, 6.0, ((0, 16),)),
        "rev_proj": bell_draw(part_splits[1], (SEQ, 3 * D), 1.0, 6.0, ((0, 16),)),
        "tokens": with_ends(jax.random.randint(part_splits[2], (SEQ,), 0, 5), jax.random.fold_in(part_splits[2], 1), 0, 4).astype(jnp.int32),
        "short_taps": bell_draw(key_of[3], (3, 3 * D), 3 ** -0.5, 3.5, (), jnp.float32),
        "long_kernel": draw_long_kernel(jax.random.fold_in(key_of[7], 71), part),
        "skip_gain": bell_draw(key_of[5], (D,), 1.0, 4.0, ((0, 16),), jnp.float32),
        "out_weight": bell_draw(key_of[6], (D, D), D ** -0.5, 0.1875),
    }


def long_filter(signal, spectrum, skip_gain):
    columns = signal.astype(jnp.float32).T
    product = jnp.fft.rfft(columns, n=2 * SEQ, axis=1) * spectrum
    filtered = jnp.fft.irfft(product, n=2 * SEQ, axis=1)[:, :SEQ]
    return (filtered + skip_gain[:, None] * columns).T.astype(jnp.bfloat16)


def reference(fwd_proj, rev_proj, tokens, short_taps, long_kernel, skip_gain, out_weight):
    fwd_rows = fwd_proj.astype(jnp.float32)
    rev_rows = rev_proj.astype(jnp.float32)
    blank = jnp.zeros((2, fwd_rows.shape[1]), jnp.float32)
    fwd_ext = jnp.concatenate([blank, fwd_rows], axis=0)
    rev_ext = jnp.concatenate([rev_rows, blank], axis=0)
    fwd_mixed = short_taps[0] * fwd_ext[2:] + short_taps[1] * fwd_ext[1:-1] + short_taps[2] * fwd_ext[:-2]
    rev_mixed = short_taps[0] * rev_ext[:-2] + short_taps[1] * rev_ext[1:-1] + short_taps[2] * rev_ext[2:]
    known = (tokens != 4).astype(jnp.float32)[:, None]
    fwd_input = (known * fwd_mixed[:, D:2 * D] * fwd_mixed[:, :D]).astype(jnp.bfloat16)
    rev_input = (known * rev_mixed[:, D:2 * D] * rev_mixed[:, :D]).astype(jnp.bfloat16)
    spectrum = jnp.fft.rfft(long_kernel, n=2 * SEQ, axis=1)
    fwd_out = long_filter(fwd_input, spectrum, skip_gain)
    rev_out = long_filter(rev_input[::-1], spectrum, skip_gain)[::-1]
    fwd_gated = fwd_mixed[:, 2 * D:] * fwd_out.astype(jnp.float32)
    rev_gated = rev_mixed[:, 2 * D:] * rev_out.astype(jnp.float32)
    combined = (fwd_gated + rev_gated[:, ::-1]).astype(jnp.bfloat16)
    return jnp.dot(combined, out_weight, preferred_element_type=jnp.float32).astype(jnp.bfloat16)
```

```python
import functools

import jax
import jax.numpy as jnp
import ml_dtypes
import numpy as np
from jax import lax
from jax.experimental import pallas as pl
from jax.experimental.pallas import tpu as pltpu
from jax.sharding import PartitionSpec as P

OUTER = 32
HALF = OUTER // 2
BINS = HALF + 1
PAIRS = (BINS + 1) // 2
EXTRA = 8
LANES = 128
TILE = 16
CHUNK = 32
BIN_GROUP = 6
VMEM_BYTES = 30 * 1024 * 1024
EDGE_LANES = 256
EDGE_ROWS = 2
FULL_VMEM_BYTES = 60000000


def split_table(table):
    high = table.astype(np.float32).astype(ml_dtypes.bfloat16)
    low = (table - high.astype(np.float64)).astype(np.float32).astype(ml_dtypes.bfloat16)
    return np.stack([high, low])


def outer_rows():
    rows = [(0, 0), (HALF, 0)]
    for bin_index in range(1, HALF):
        rows += [(bin_index, 0), (bin_index, 1)]
    return rows


def dft_tables(length):
    inner = length // HALF
    total = 2 * length
    blocks = np.arange(HALF)
    enter = np.zeros((OUTER, HALF))
    for row, (bin_index, part) in enumerate(outer_rows()):
        phase = 2.0 * np.pi * (bin_index * blocks % OUTER) / OUTER
        enter[row] = -np.sin(phase) if part else np.cos(phase)
    angles = 2.0 * np.pi * (np.outer(np.arange(inner), np.arange(inner)) % inner) / inner
    cos, sin = np.cos(angles), np.sin(angles)
    mix = np.block([[cos, sin], [-sin, cos]])
    turn = np.zeros((inner, LANES))
    turn_phase = 2.0 * np.pi * np.outer(np.arange(inner), np.arange(BINS)) / total
    turn[:, :BINS] = np.cos(turn_phase)
    turn[:, LANES // 2 : LANES // 2 + BINS] = np.sin(turn_phase)
    core = np.repeat(split_table(enter).astype(np.float32), TILE, axis=2)
    return (
        core,
        split_table(mix),
        turn.astype(np.float32),
    )


def dot(left, right):
    return jnp.dot(left, right, preferred_element_type=jnp.float32)


def table_dot(table_ref, right):
    return dot(table_ref[0], right) + dot(table_ref[1], right)


def lanes_of(shape):
    return lax.broadcasted_iota(jnp.int32, shape, len(shape) - 1)


def swap(value):
    lanes = value.shape[1]
    if lanes == LANES:
        return pltpu.roll(value, lanes // 2, 1)
    return jnp.concatenate([value[:, lanes // 2 :], value[:, : lanes // 2]], axis=1)


def left_halves(one, two):
    value = one if one is not None else two
    left = lanes_of(value.shape) < value.shape[1] // 2
    one = jnp.zeros_like(value) if one is None else one
    two = jnp.zeros_like(value) if two is None else swap(two)
    return jnp.where(left, one, two)


def right_halves(one, two):
    value = one if one is not None else two
    left = lanes_of(value.shape) < value.shape[1] // 2
    one = jnp.zeros_like(value) if one is None else swap(one)
    two = jnp.zeros_like(value) if two is None else two
    return jnp.where(left, one, two)


def slot(bin_index, part):
    if bin_index >= BINS or (part and bin_index in (0, HALF)):
        return None
    if bin_index in (0, HALF):
        return bin_index // HALF
    return 2 * bin_index + part


def enter_stage(load, dots, turn_ref, per, half_rows, put):
    inner = 2 * per * half_rows
    for group in range(per):
        for tile in range(0, half_rows // TILE, 2):
            pair = [load(group, tile), load(group, tile + 1)]
            lanes = pair[0].shape[1]
            section = dots(jnp.concatenate(pair, axis=1))
            for which in range(2):
                by_row = section[:, which * lanes : (which + 1) * lanes].reshape(OUTER, TILE, lanes)

                def part_of(bin_index, part):
                    row = slot(bin_index, part)
                    return None if row is None else by_row[row]

                for index in range(PAIRS):
                    bins = (2 * index, 2 * index + 1)
                    reals = [part_of(b, 0) for b in bins]
                    imags = [part_of(b, 1) for b in bins]
                    for side, halves in enumerate((left_halves, right_halves)):
                        start = (2 * group + side) * half_rows + (tile + which) * TILE
                        cos = turn_ref[index, 0, start : start + TILE, :]
                        sin = turn_ref[index, 1, start : start + TILE, :]
                        real = halves(*reals)
                        if imags[0] is None and imags[1] is None:
                            put(index, start, real * cos)
                            put(index, inner + start, real * -sin)
                        else:
                            imag = halves(*imags)
                            put(index, start, real * cos + imag * sin)
                            put(index, inner + start, imag * cos - real * sin)


def expand(core, target):
    row = lax.broadcasted_iota(jnp.int32, (TILE, core.shape[1]), 0)
    same = row == lanes_of(row.shape) % TILE
    for index in range(OUTER):
        wide = jnp.broadcast_to(core[index : index + 1], row.shape)
        target[index * TILE : (index + 1) * TILE, :] = jnp.where(same, wide, 0.0).astype(jnp.bfloat16)


def turn_pair(turn_ref, start, count, bin_index, lanes):
    rows = pl.ds(start, count)
    cos = jnp.broadcast_to(turn_ref[rows, bin_index : bin_index + 1], (count, lanes))
    at = LANES // 2 + bin_index
    sin = jnp.broadcast_to(turn_ref[rows, at : at + 1], (count, lanes))
    return cos, sin


def store_sections(section, turn_ref, tile, lanes, put):
    start = tile * TILE
    by_row = section.reshape(OUTER, TILE, lanes)
    for bin_index in range(BINS):
        cos, sin = turn_pair(turn_ref, start, TILE, bin_index, lanes)
        if bin_index in (0, HALF):
            real = by_row[0 if bin_index == 0 else 1]
            put(bin_index, start, real * cos, real * -sin)
        else:
            real = by_row[2 * bin_index]
            imag = by_row[2 * bin_index + 1]
            put(bin_index, start, real * cos + imag * sin, imag * cos - real * sin)


def short_filter(value, taps, later, near=None):
    rows = value.shape[0]
    row = lax.broadcasted_iota(jnp.int32, (EXTRA, LANES), 0)
    shifted = []
    for lag in (1, 2):
        moved = pltpu.roll(value, rows - lag if later else lag, 0)
        shift = EXTRA - lag if later else lag
        fill = 0.0 if near is None else pltpu.roll(near, shift, 0)
        if later:
            tail = jnp.where(row < EXTRA - lag, moved[rows - EXTRA :], fill)
            moved = jnp.concatenate([moved[: rows - EXTRA], tail], axis=0)
        else:
            head = jnp.where(row >= lag, moved[:EXTRA], fill)
            moved = jnp.concatenate([head, moved[EXTRA:]], axis=0)
        shifted.append(moved)
    return taps[0:1] * value + taps[1:2] * shifted[0] + taps[2:3] * shifted[1]


def chunk_filter(ref, start, columns, taps, later):
    end = start + CHUNK
    value = ref[start:end, columns].astype(jnp.float32)
    near = None
    if later and end < ref.shape[0]:
        near = ref[end : end + TILE, columns].astype(jnp.float32)[:EXTRA]
    elif not later and start > 0:
        near = ref[start - TILE : start, columns].astype(jnp.float32)[EXTRA:]
    return short_filter(value, taps, later, near)


def gate_kernel(
    fwd_hbm, rev_hbm, tokens_hbm, taps_hbm, out_hbm, fwd_o_hbm, rev_o_hbm,
    fwd_ref, rev_ref, fwd_edge_ref, rev_edge_ref, tokens_ref, taps_ref, out_ref, fwd_o_ref, rev_o_ref,
    first_q_ref, sems, small_sems, out_sems
):
    rows = fwd_ref.shape[0]
    width = fwd_ref.shape[1] // 2
    lanes = out_ref.shape[2]
    count = lanes // 2
    small = [
        pltpu.make_async_copy(taps_hbm, taps_ref, small_sems.at[0]),
        pltpu.make_async_copy(tokens_hbm, tokens_ref, small_sems.at[1]),
        pltpu.make_async_copy(
            fwd_hbm.at[pl.ds(rows - TILE, TILE), pl.ds(2 * width, width)],
            fwd_edge_ref,
            small_sems.at[2],
        ),
        pltpu.make_async_copy(
            rev_hbm.at[pl.ds(0, TILE), pl.ds(2 * width, width)], rev_edge_ref, small_sems.at[3]
        ),
    ]
    loads, stores = [], []
    for step in range(rows // CHUNK):
        part = (pl.ds(step * CHUNK, CHUNK), pl.ds(0, 2 * width))
        copies = [
            pltpu.make_async_copy(fwd_hbm.at[part], fwd_ref.at[part], sems.at[step, 0]),
            pltpu.make_async_copy(rev_hbm.at[part], rev_ref.at[part], sems.at[step, 1]),
        ]
        for copy in copies:
            copy.start()
        loads.append(copies)
        if step == 0:
            for copy in small:
                copy.start()
    for copy in small:
        copy.wait()
    known_row = jnp.where(tokens_ref[...] != 4, 1.0, 0.0).astype(jnp.float32)
    known = jnp.transpose(jnp.broadcast_to(known_row, (LANES, rows)))
    edge_row = lax.broadcasted_iota(jnp.int32, (EXTRA, LANES), 0)

    def piece_of(left, right, piece):
        left_shift = (LANES - piece * count) % LANES
        right_shift = (LANES + count - piece * count) % LANES
        left = pltpu.roll(left, left_shift, 1) if left_shift else left
        right = pltpu.roll(right, right_shift, 1) if right_shift else right
        return jnp.where(lanes_of(left.shape) < count, left, right)[:, :lanes].astype(jnp.bfloat16)

    def rows_of(ref, columns, start):
        return ref[start : start + TILE, columns].astype(jnp.float32)

    def with_rows(edge, rows_at, value, at):
        moved = pltpu.roll(value, (rows_at - at) % EXTRA, 0)
        return jnp.where((edge_row >= rows_at) & (edge_row < rows_at + 2), moved, edge)

    pieces = LANES // count
    for copy in loads[0]:
        copy.wait()
    for step in range(rows // CHUNK):
        start = step * CHUNK
        final = start + CHUNK == rows
        if not final:
            for copy in loads[step + 1]:
                copy.wait()
        here = slice(start, start + CHUNK)
        for block in range(width // LANES):
            low = block * LANES
            at_v = slice(low, low + LANES)
            at_q = slice(width + low, width + low + LANES)
            taps_v, taps_q = taps_ref[:, at_v], taps_ref[:, at_q]
            fwd_v = chunk_filter(fwd_ref, start, at_v, taps_v, False)
            fwd_q = chunk_filter(fwd_ref, start, at_q, taps_q, False)
            fwd_body = known[here] * fwd_q * fwd_v
            rev_v = chunk_filter(rev_ref, start, at_v, taps_v, True)
            rev_q = chunk_filter(rev_ref, start, at_q, taps_q, True)
            rev_body = known[here] * rev_q * rev_v
            if start == 0:
                part = jnp.where(known[:EXTRA] > 0.0, fwd_v[:EXTRA], jnp.inf)
                head = jnp.where(edge_row < 2, part, fwd_body[:EXTRA])
                fwd_body = jnp.concatenate([head, fwd_body[EXTRA:]], axis=0)
                first_q_ref[:, at_v] = fwd_q[:EXTRA]
            if final:
                part = jnp.where(known[rows - EXTRA :] > 0.0, rev_v[CHUNK - EXTRA :], jnp.inf)
                tail = jnp.where(edge_row >= EXTRA - 2, part, rev_body[CHUNK - EXTRA :])
                rev_body = jnp.concatenate([rev_body[: CHUNK - EXTRA], tail], axis=0)
                raw_o = rows_of(fwd_edge_ref, at_v, 0)[EXTRA:]
                edge = jnp.where(edge_row < 2, first_q_ref[:, at_v], raw_o)
                edge = with_rows(edge, 2, rows_of(fwd_ref, at_v, rows - TILE)[EXTRA:], 6)
                edge = with_rows(edge, 4, rows_of(fwd_ref, at_q, rows - TILE)[EXTRA:], 6)
                fwd_body = jnp.concatenate([fwd_body, edge], axis=0)
                place = (
                    slice(low // EDGE_LANES * EDGE_ROWS, (low // EDGE_LANES + 1) * EDGE_ROWS),
                    slice(low % EDGE_LANES, low % EDGE_LANES + LANES),
                )
                fwd_o_ref[place] = pltpu.roll(raw_o, 2, 0)[:EDGE_ROWS]
                raw_o = rows_of(rev_edge_ref, at_v, 0)[:EXTRA]
                edge = jnp.where(edge_row < 2, pltpu.roll(rev_q[CHUNK - EXTRA :], 2, 0), 0.0)
                edge = with_rows(edge, 2, rows_of(rev_ref, at_v, 0)[:EXTRA], 0)
                edge = with_rows(edge, 4, rows_of(rev_ref, at_q, 0)[:EXTRA], 0)
                rev_body = jnp.concatenate([rev_body, edge], axis=0)
                rev_o_ref[place] = raw_o[:EDGE_ROWS]
            for piece in range(pieces):
                out_ref[block * pieces + piece, start : start + fwd_body.shape[0], :] = piece_of(
                    fwd_body, rev_body, piece
                )
        part = (slice(None), pl.ds(start, CHUNK + (EXTRA if final else 0)))
        copy = pltpu.make_async_copy(out_ref.at[part], out_hbm.at[part], out_sems.at[step])
        copy.start()
        stores.append(copy)
    for at, (source, target) in enumerate(((fwd_o_ref, fwd_o_hbm), (rev_o_ref, rev_o_hbm))):
        copy = pltpu.make_async_copy(source, target, small_sems.at[4 + at])
        copy.start()
        stores.append(copy)
    for copy in stores:
        copy.wait()


def sections_kernel(
    me_ref, kernel_hbm, skip_hbm, taps_hbm, core_hbm, phase_hbm,
    high, low, own_taps_ref, core_ref, phase_ref,
    kernel_ref, skip_ref, taps_ref, wide_ref, enter_ref, turn_ref, signal, sems
):
    moves = (
        (phase_hbm, phase_ref), (kernel_hbm, kernel_ref), (skip_hbm, skip_ref),
        (taps_hbm, taps_ref), (core_hbm, wide_ref), (core_hbm.at[0], core_ref),
    )
    copies = [
        pltpu.make_async_copy(source, target, sems.at[at])
        for at, (source, target) in enumerate(moves)
    ]
    for copy in copies:
        copy.start()
    count, length = kernel_ref.shape
    lanes = 2 * count
    inner = length // HALF
    half_rows = signal.shape[2]
    rows = 2 * half_rows
    per = inner // rows
    width = taps_ref.shape[1] // 3

    copies[0].wait()
    for index in range(PAIRS):
        for part in range(2):
            columns = [part * (LANES // 2) + min(2 * index + b, BINS) for b in range(2)]
            sides = [
                jnp.broadcast_to(phase_ref[:, column : column + 1], (inner, lanes))
                for column in columns
            ]
            turn_ref[index, part] = jnp.where(lanes_of((inner, lanes)) < count, *sides)

    for copy in copies[1:5]:
        copy.wait()
    me = me_ref[0]
    per_block = LANES // count
    block = me // per_block
    shift = lax.rem(LANES - (me - block * per_block) * count, LANES)
    for which in range(2):
        column = pl.multiple_of(which * width + block * LANES, LANES)
        own = pltpu.roll(taps_ref[:, pl.ds(column, LANES)], shift, 1)
        both = jnp.where(lanes_of(own.shape) < count, own, pltpu.roll(own, count, 1))[:, :lanes]
        for tap in range(3):
            own_taps_ref[3 * which + tap : 3 * which + tap + 1, :] = both[tap : tap + 1]
    own_taps_ref[6:8, :] = jnp.zeros((2, lanes), jnp.float32)

    for start in range(0, length, rows):
        piece = kernel_ref[:, start : start + rows]
        both = jnp.concatenate([piece, pltpu.roll(piece, half_rows, 1)], axis=0)
        turned = jnp.transpose(both)[:half_rows]
        if start == 0:
            gain = skip_ref[...]
            gains = jnp.concatenate([gain, jnp.zeros_like(gain)], axis=1)
            row = lax.broadcasted_iota(jnp.int32, turned.shape, 0)
            turned = turned + jnp.where(row == 0, gains, 0.0)
        signal[start // inner, start % inner // rows] = turned

    def load(group, tile):
        return signal[:, group, tile * TILE : (tile + 1) * TILE, :].reshape(HALF * TILE, lanes)

    def enter_dots(value):
        top = value.astype(jnp.bfloat16)
        rest = (value - top.astype(jnp.float32)).astype(jnp.bfloat16)
        return table_dot(enter_ref, top) + dot(enter_ref[0], rest)

    def put(index, start, value):
        top = value.astype(jnp.bfloat16)
        high[index, start : start + TILE, :] = top
        low[index, start : start + TILE, :] = (value - top.astype(jnp.float32)).astype(jnp.bfloat16)

    for part in range(2):
        expand(wide_ref[part], enter_ref.at[part])
    enter_stage(load, enter_dots, turn_ref, per, half_rows, put)
    copies[5].wait()


def spectrum_kernel(high, low, mix_hbm, *refs):
    *spec_refs, mix_out_ref, mix_ref, sems = refs
    copies = [
        pltpu.make_async_copy(mix_hbm, mix_ref, sems.at[0]),
        pltpu.make_async_copy(mix_hbm.at[0], mix_out_ref, sems.at[1]),
    ]
    for copy in copies:
        copy.start()
    for copy in copies:
        copy.wait()
    inner = high.shape[1] // 2
    lanes = high.shape[2]
    count = lanes // 2
    length = inner * HALF
    for first in range(0, PAIRS, 2):
        group = range(first, min(first + 2, PAIRS))
        top = jnp.concatenate([high[index] for index in group], axis=1)
        rest = jnp.concatenate([low[index] for index in group], axis=1)
        spec = table_dot(mix_ref, top) + dot(mix_ref[0], rest)
        for at, index in enumerate(group):
            pair = spec[:, at * lanes : (at + 1) * lanes]
            left = lanes_of((inner, lanes)) < count
            for side in range(2):
                if 2 * index + side == BINS:
                    break
                for part in range(2):
                    here = pair[part * inner : (part + 1) * inner]
                    there = swap(here)
                    value = jnp.where(left, there, here) if side else jnp.where(left, here, there)
                    if part:
                        value = jnp.where(left, value, -value)
                    weight = (1.0 if 2 * index + side in (0, HALF) else 2.0) / (2 * length)
                    value = value * weight
                    which, place = divmod(2 * index + side, BIN_GROUP)
                    spec_refs[which][place, part * inner : (part + 1) * inner, :] = value


def mended_tiles(recv_ref, own_taps_ref, group, rows):
    blocks, per, _, lanes = recv_ref.shape
    count = lanes // 2
    taps = own_taps_ref[...]
    edge = recv_ref[:, group, rows : rows + EXTRA, :].astype(jnp.float32)
    blank = jnp.zeros((1, EXTRA, lanes), jnp.float32)
    if group > 0:
        before = recv_ref[:, group - 1, rows : rows + EXTRA, :].astype(jnp.float32)
    else:
        shifted = recv_ref[: blocks - 1, per - 1, rows : rows + EXTRA, :].astype(jnp.float32)
        before = jnp.concatenate([blank, shifted], axis=0)
    if group < per - 1:
        after = recv_ref[:, group + 1, rows : rows + EXTRA, :].astype(jnp.float32)
    else:
        shifted = recv_ref[1:, 0, rows : rows + EXTRA, :].astype(jnp.float32)
        after = jnp.concatenate([shifted, blank], axis=0)
    row = lax.broadcasted_iota(jnp.int32, (EXTRA, lanes), 0)
    lane = lax.broadcasted_iota(jnp.int32, (EXTRA, lanes), 1)
    first, last = [], []
    for block in range(blocks):
        top = recv_ref[block, group, :TILE, :].astype(jnp.float32)
        part = top[:EXTRA]
        near = before[block]
        mix_v = part + taps[2:3] * pltpu.roll(near, 6, 0)
        mix_v = mix_v + jnp.where(row == 0, taps[1:2] * pltpu.roll(near, 5, 0), 0.0)
        mix_q = edge[block] + taps[5:6] * pltpu.roll(near, 4, 0)
        mix_q = mix_q + jnp.where(row == 0, taps[4:5] * pltpu.roll(near, 3, 0), 0.0)
        fixed = jnp.where(part == jnp.inf, 0.0, mix_q * mix_v)
        fixed = jnp.where((row < 2) & (lane < count), fixed, part)
        first.append(jnp.concatenate([fixed, top[EXTRA:]], axis=0).astype(jnp.bfloat16))

        end = recv_ref[block, group, rows - TILE : rows, :].astype(jnp.float32)
        part = end[EXTRA:]
        near = after[block]
        mix_v = part + taps[2:3] * pltpu.roll(near, 4, 0)
        mix_v = mix_v + jnp.where(row == 7, taps[1:2] * pltpu.roll(near, 5, 0), 0.0)
        mix_q = pltpu.roll(edge[block], 6, 0) + taps[5:6] * pltpu.roll(near, 2, 0)
        mix_q = mix_q + jnp.where(row == 7, taps[4:5] * pltpu.roll(near, 3, 0), 0.0)
        fixed = jnp.where(part == jnp.inf, 0.0, mix_q * mix_v)
        fixed = jnp.where((row >= 6) & (lane >= count), fixed, part)
        last.append(jnp.concatenate([end[:EXTRA], fixed], axis=0).astype(jnp.bfloat16))
    return jnp.stack(first), jnp.stack(last)


def filter_kernel(recv_ref, own_taps_ref, core_ref, turn_ref, *refs):
    *spec_refs, mix_ref, out_ref, sections, returned, enter_ref = refs
    expand(core_ref[...], enter_ref)
    blocks, per, padded, lanes = recv_ref.shape
    rows = padded - EXTRA
    inner = per * rows
    tiles = rows // TILE

    def put(bin_index, start, real, imag):
        sections[bin_index, start : start + TILE, :] = real.astype(jnp.bfloat16)
        sections[bin_index, inner + start : inner + start + TILE, :] = imag.astype(jnp.bfloat16)

    for group in range(per):
        first, last = mended_tiles(recv_ref, own_taps_ref, group, rows)
        loaded = [first]
        for tile in range(1, tiles - 1):
            loaded.append(recv_ref[:, group, tile * TILE : (tile + 1) * TILE, :])
        loaded.append(last)
        loaded = [value.reshape(blocks * TILE, lanes) for value in loaded]
        def section_of(tile):
            return dot(enter_ref[...], jnp.concatenate(loaded[tile : tile + 2], axis=1))

        ahead = section_of(0)
        for tile in range(0, tiles, 2):
            section = ahead
            if tile + 2 < tiles:
                ahead = section_of(tile + 2)
            at = group * tiles + tile
            store_sections(section[:, :lanes], turn_ref, at, lanes, put)
            store_sections(section[:, lanes:], turn_ref, at + 1, lanes, put)

    def bins_from(first):
        return range(first, min(first + 2, BINS))

    def spec_of(first):
        pair = [sections[b] for b in bins_from(first)]
        return dot(mix_ref[...], jnp.concatenate(pair, axis=1))

    def back_of(first, spec):
        gains = [spec_refs[b // BIN_GROUP][b % BIN_GROUP] for b in bins_from(first)]
        gain = jnp.concatenate(gains, axis=1)
        real, imag = spec[:inner], spec[inner:]
        gain_real, gain_imag = gain[:inner], gain[inner:]
        product = jnp.concatenate(
            [real * gain_real - imag * gain_imag, -real * gain_imag - imag * gain_real], axis=0
        ).astype(jnp.bfloat16)
        return dot(mix_ref[...], product)

    def store_returned(first, back):
        for at, b in enumerate(bins_from(first)):
            real = back[:inner, at * lanes : (at + 1) * lanes]
            imag = back[inner:, at * lanes : (at + 1) * lanes]
            cos, sin = turn_pair(turn_ref, 0, inner, b, lanes)
            returned[slot(b, 0)] = (real * cos + imag * sin).astype(jnp.bfloat16)
            if b not in (0, HALF):
                returned[slot(b, 1)] = (real * sin - imag * cos).astype(jnp.bfloat16)

    ahead, behind = spec_of(0), None
    for first in range(0, BINS, 2):
        spec = ahead
        if first + 2 < BINS:
            ahead = spec_of(first + 2)
        back = back_of(first, spec)
        if behind is not None:
            store_returned(first - 2, behind)
        behind = back
    store_returned(BINS - 1, behind)

    leave = jnp.transpose(enter_ref[...])
    for tile in range(0, inner // TILE, 2):
        pair = jnp.concatenate(
            [
                returned[:, at * TILE : (at + 1) * TILE, :].reshape(OUTER * TILE, lanes)
                for at in (tile, tile + 1)
            ],
            axis=1,
        )
        value = dot(leave, pair).astype(jnp.bfloat16)
        group, place = divmod(tile, tiles)
        for at in (0, 1):
            start = (place + at) * TILE
            out_ref[:, group, start : start + TILE, :] = value[
                :, at * lanes : (at + 1) * lanes
            ].reshape(blocks, TILE, lanes)


def mixing_kernel(
    ret_ref, fwd_o_ref, rev_o_ref, fwd_ref, rev_ref, taps_ref, weight_ref, out_ref, combined, total
):
    rows = fwd_ref.shape[0]
    width = weight_ref.shape[0]
    count = ret_ref.shape[2] // 2
    pieces = LANES // count
    blocks = width // LANES
    edge_row = lax.broadcasted_iota(jnp.int32, (EXTRA, LANES), 0)
    mirror = LANES - 1 - lax.broadcasted_iota(jnp.int32, (rows, LANES), 1)

    def near_edge(edges, block, target):
        low = block * LANES
        at_row = low // EDGE_LANES * EDGE_ROWS
        start = at_row // EXTRA * EXTRA
        at_lane = low % EDGE_LANES
        tile = edges[start : start + EXTRA, at_lane : at_lane + LANES]
        shift = (target - at_row + start) % EXTRA
        return pltpu.roll(tile, shift, 0) if shift else tile

    def columns(block, which):
        chunks = [
            ret_ref[block * pieces + piece].astype(jnp.float32)[
                :, which * count : (which + 1) * count
            ]
            for piece in range(pieces)
        ]
        return jnp.concatenate(chunks, axis=1)

    for block in range(blocks):
        low = 2 * width + block * LANES
        taps = taps_ref[:, low : low + LANES]
        mixed = short_filter(fwd_ref[:, low : low + LANES].astype(jnp.float32), taps, False)
        more = jnp.where(edge_row < 2, taps[2:3] * near_edge(fwd_o_ref, block, 0), 0.0)
        last = jnp.where(edge_row == 0, taps[1:2] * near_edge(fwd_o_ref, block, -1), 0.0)
        mixed = jnp.concatenate([mixed[:EXTRA] + more + last, mixed[EXTRA:]], axis=0)
        gated = mixed * columns(block, 0)

        other = blocks - 1 - block
        low = 2 * width + other * LANES
        taps = taps_ref[:, low : low + LANES]
        mixed = short_filter(rev_ref[:, low : low + LANES].astype(jnp.float32), taps, True)
        more = jnp.where(edge_row >= 6, taps[2:3] * near_edge(rev_o_ref, other, 6), 0.0)
        first = jnp.where(edge_row == 7, taps[1:2] * near_edge(rev_o_ref, other, 7), 0.0)
        tail = mixed[rows - EXTRA :] + more + first
        mixed = jnp.concatenate([mixed[: rows - EXTRA], tail], axis=0)
        turned = jnp.take_along_axis(mixed * columns(other, 1), mirror, axis=1)
        combined[:, block * LANES : (block + 1) * LANES] = (gated + turned).astype(jnp.bfloat16)
        if block % 2:
            part = slice((block - 1) * LANES, (block + 1) * LANES)
            product = dot(combined[:, part], weight_ref[part, :])
            if block == 1:
                total[...] = product
            elif block < blocks - 1:
                total[...] += product
            else:
                out_ref[...] = (total[...] + product).astype(jnp.bfloat16)


HBM = pl.BlockSpec(memory_space=pltpu.HBM)
VMEM = pl.BlockSpec(memory_space=pltpu.VMEM)
SMEM = pl.BlockSpec(memory_space=pltpu.SMEM)


def params(limit=VMEM_BYTES):
    return pltpu.CompilerParams(vmem_limit_bytes=limit)


def cost(flops, size):
    return pl.CostEstimate(flops=flops, bytes_accessed=size, transcendentals=0)


def exchange(value):
    return lax.all_to_all(value, "ctx", split_axis=0, concat_axis=0, tiled=True)


def shifted(value, steps):
    count = lax.axis_size("ctx")
    first, end = max(0, -steps), min(count, count - steps)
    return lax.ppermute(value, "ctx", [(source, source + steps) for source in range(first, end)])


def per_device(fwd_proj, rev_proj, tokens, short_taps, long_kernel, skip_gain, out_weight):
    rows = fwd_proj.shape[0]
    half_rows = rows // 2
    width = fwd_proj.shape[1] // 3
    count, length = long_kernel.shape
    devices = length // rows
    lanes = 2 * count
    inner = length // HALF
    per = devices // HALF
    padded = rows + EXTRA
    edge_block = (EDGE_ROWS * width // EDGE_LANES, EDGE_LANES)
    tables = [jnp.asarray(table) for table in dft_tables(length)]
    core, mix, phases = tables
    outer_shape = (OUTER * TILE, HALF * TILE)
    block = (devices, padded, lanes)

    sent, fwd_o, rev_o = pl.pallas_call(
        gate_kernel,
        out_shape=(
            jax.ShapeDtypeStruct(block, jnp.bfloat16),
            jax.ShapeDtypeStruct(edge_block, jnp.float32),
            jax.ShapeDtypeStruct(edge_block, jnp.float32),
        ),
        in_specs=[HBM] * 4,
        out_specs=(HBM,) * 3,
        scratch_shapes=[
            pltpu.VMEM((rows, 2 * width), jnp.bfloat16),
            pltpu.VMEM((rows, 2 * width), jnp.bfloat16),
            pltpu.VMEM((TILE, width), jnp.bfloat16),
            pltpu.VMEM((TILE, width), jnp.bfloat16),
            pltpu.VMEM((1, rows), jnp.int32),
            pltpu.VMEM(short_taps.shape, jnp.float32),
            pltpu.VMEM(block, jnp.bfloat16),
            pltpu.VMEM(edge_block, jnp.float32),
            pltpu.VMEM(edge_block, jnp.float32),
            pltpu.VMEM((EXTRA, width), jnp.float32),
            pltpu.SemaphoreType.DMA((rows // CHUNK, 2)),
            pltpu.SemaphoreType.DMA((6,)),
            pltpu.SemaphoreType.DMA((rows // CHUNK,)),
        ],
        compiler_params=params(FULL_VMEM_BYTES),
        name="gate",
    )(fwd_proj, rev_proj, tokens.reshape(1, rows), short_taps)


    me = lax.axis_index("ctx").astype(jnp.int32).reshape(1)
    sent, me = lax.optimization_barrier((sent, me))
    received = exchange(sent)
    section_shape = jax.ShapeDtypeStruct((PAIRS, 2 * inner, lanes), jnp.bfloat16)
    spectrum_cost = cost(3 * PAIRS * 2 * (2 * inner) ** 2 * lanes, 4 * 1024 * 1024)
    high, low, own_taps, own_core, own_phases = pl.pallas_call(
        sections_kernel,
        out_shape=(
            section_shape,
            section_shape,
            jax.ShapeDtypeStruct((8, lanes), jnp.float32),
            jax.ShapeDtypeStruct(core.shape[1:], jnp.float32),
            jax.ShapeDtypeStruct(phases.shape, jnp.float32),
        ),
        in_specs=[SMEM] + [HBM] * 5,
        out_specs=(VMEM,) * 5,
        scratch_shapes=[
            pltpu.VMEM((count, length), jnp.float32),
            pltpu.VMEM((1, count), jnp.float32),
            pltpu.VMEM(short_taps.shape, jnp.float32),
            pltpu.VMEM(core.shape, jnp.float32),
            pltpu.VMEM((2,) + outer_shape, jnp.bfloat16),
            pltpu.VMEM((PAIRS, 2, inner, lanes), jnp.float32),
            pltpu.VMEM((HALF, per, half_rows, lanes), jnp.float32),
            pltpu.SemaphoreType.DMA((6,)),
        ],
        compiler_params=params(),
        cost_estimate=spectrum_cost,
        name="sections",
    )(me, long_kernel, skip_gain.reshape(1, count), short_taps, core, phases)

    own_taps, fwd_o, rev_o = lax.optimization_barrier((own_taps, fwd_o, rev_o))
    fwd_o = shifted(fwd_o, 1)
    rev_o = shifted(rev_o, -1)
    own_taps, fwd_o, rev_o = lax.optimization_barrier((own_taps, fwd_o, rev_o))

    groups = [min(BIN_GROUP, BINS - first) for first in range(0, BINS, BIN_GROUP)]
    spectrum = pl.pallas_call(
        spectrum_kernel,
        out_shape=tuple(
            jax.ShapeDtypeStruct((group, 2 * inner, lanes), jnp.float32) for group in groups
        )
        + (jax.ShapeDtypeStruct(mix.shape[1:], jnp.bfloat16),),
        in_specs=[VMEM, VMEM, HBM],
        out_specs=(VMEM,) * (len(groups) + 1),
        scratch_shapes=[
            pltpu.VMEM(mix.shape, jnp.bfloat16),
            pltpu.SemaphoreType.DMA((2,)),
        ],
        compiler_params=params(),
        cost_estimate=spectrum_cost,
        name="spectrum",
    )(high, low, mix)

    filtered = pl.pallas_call(
        filter_kernel,
        out_shape=jax.ShapeDtypeStruct((HALF, per, rows, lanes), jnp.bfloat16),
        in_specs=[VMEM] * (4 + len(spectrum)),
        out_specs=VMEM,
        scratch_shapes=[
            pltpu.VMEM((BINS, 2 * inner, lanes), jnp.bfloat16),
            pltpu.VMEM((OUTER, inner, lanes), jnp.bfloat16),
            pltpu.VMEM(outer_shape, jnp.bfloat16),
        ],
        compiler_params=params(),
        cost_estimate=cost(4 * PAIRS * 4 * (2 * inner) ** 2 * lanes, 4 * 1024 * 1024),
        name="filter",
    )(received.reshape(HALF, per, padded, lanes), own_taps, own_core, own_phases, *spectrum)

    returned = exchange(filtered.reshape(devices, rows, lanes))

    return pl.pallas_call(
        mixing_kernel,
        out_shape=jax.ShapeDtypeStruct((rows, width), jnp.bfloat16),
        in_specs=[VMEM] * 7,
        out_specs=VMEM,
        scratch_shapes=[
            pltpu.VMEM((rows, width), jnp.bfloat16),
            pltpu.VMEM((rows, width), jnp.float32),
        ],
        compiler_params=params(),
        cost_estimate=cost(2 * rows * width * width, 4 * 1024 * 1024),
        name="mixing",
    )(returned, fwd_o, rev_o, fwd_proj, rev_proj, short_taps, out_weight)


def solution(mesh):
    in_specs = (
        P(("dp", "ctx"), None),
        P(("dp", "ctx"), None),
        P(("dp", "ctx")),
        P(),
        P("ctx", None),
        P("ctx"),
        P(),
    )
    out_specs = P(("dp", "ctx"), None)
    return jax.shard_map(
        per_device, mesh=mesh, in_specs=in_specs, out_specs=out_specs, check_vma=False
    )
```

```python
import functools

import jax
import jax.numpy as jnp
import ml_dtypes
import numpy as np
from jax import lax
from jax.experimental import pallas as pl
from jax.experimental.pallas import tpu as pltpu
from jax.sharding import PartitionSpec as P

OUTER = 32
HALF = OUTER // 2
BINS = HALF + 1
PAIRS = (BINS + 1) // 2
EXTRA = 8
LANES = 128
TILE = 16
CHUNK = 32
BIN_GROUP = 2
VMEM_BYTES = 30 * 1024 * 1024
EDGE_LANES = 256
EDGE_ROWS = 2
FULL_VMEM_BYTES = 60000000


def split_table(table):
    high = table.astype(np.float32).astype(ml_dtypes.bfloat16)
    low = (table - high.astype(np.float64)).astype(np.float32).astype(ml_dtypes.bfloat16)
    return np.stack([high, low])


def outer_rows():
    rows = [(0, 0), (HALF, 0)]
    for bin_index in range(1, HALF):
        rows += [(bin_index, 0), (bin_index, 1)]
    return rows


def dft_tables(length):
    inner = length // HALF
    total = 2 * length
    blocks = np.arange(HALF)
    enter = np.zeros((OUTER, HALF))
    for row, (bin_index, part) in enumerate(outer_rows()):
        phase = 2.0 * np.pi * (bin_index * blocks % OUTER) / OUTER
        enter[row] = -np.sin(phase) if part else np.cos(phase)
    angles = 2.0 * np.pi * (np.outer(np.arange(inner), np.arange(inner)) % inner) / inner
    cos, sin = np.cos(angles), np.sin(angles)
    mix = np.block([[cos, sin], [-sin, cos]])
    turn = np.zeros((inner, LANES))
    turn_phase = 2.0 * np.pi * np.outer(np.arange(inner), np.arange(BINS)) / total
    turn[:, :BINS] = np.cos(turn_phase)
    turn[:, LANES // 2 : LANES // 2 + BINS] = np.sin(turn_phase)
    core = np.repeat(split_table(enter).astype(np.float32), TILE, axis=2)
    return (
        core,
        split_table(mix),
        turn.astype(np.float32),
    )


def dot(left, right):
    return jnp.dot(left, right, preferred_element_type=jnp.float32)


def table_dot(table_ref, right):
    return dot(table_ref[0], right) + dot(table_ref[1], right)


def lanes_of(shape):
    return lax.broadcasted_iota(jnp.int32, shape, len(shape) - 1)


def swap(value):
    lanes = value.shape[1]
    if lanes == LANES:
        return pltpu.roll(value, lanes // 2, 1)
    return jnp.concatenate([value[:, lanes // 2 :], value[:, : lanes // 2]], axis=1)


def left_halves(one, two):
    value = one if one is not None else two
    left = lanes_of(value.shape) < value.shape[1] // 2
    one = jnp.zeros_like(value) if one is None else one
    two = jnp.zeros_like(value) if two is None else swap(two)
    return jnp.where(left, one, two)


def right_halves(one, two):
    value = one if one is not None else two
    left = lanes_of(value.shape) < value.shape[1] // 2
    one = jnp.zeros_like(value) if one is None else swap(one)
    two = jnp.zeros_like(value) if two is None else two
    return jnp.where(left, one, two)


def slot(bin_index, part):
    if bin_index >= BINS or (part and bin_index in (0, HALF)):
        return None
    if bin_index in (0, HALF):
        return bin_index // HALF
    return 2 * bin_index + part


def enter_stage(load, dots, turn_ref, per, half_rows, put):
    inner = 2 * per * half_rows
    for group in range(per):
        for tile in range(0, half_rows // TILE, 2):
            pair = [load(group, tile), load(group, tile + 1)]
            lanes = pair[0].shape[1]
            section = dots(jnp.concatenate(pair, axis=1))
            for which in range(2):
                by_row = section[:, which * lanes : (which + 1) * lanes].reshape(OUTER, TILE, lanes)

                def part_of(bin_index, part):
                    row = slot(bin_index, part)
                    return None if row is None else by_row[row]

                for index in range(PAIRS):
                    bins = (2 * index, 2 * index + 1)
                    reals = [part_of(b, 0) for b in bins]
                    imags = [part_of(b, 1) for b in bins]
                    for side, halves in enumerate((left_halves, right_halves)):
                        start = (2 * group + side) * half_rows + (tile + which) * TILE
                        cos = turn_ref[index, 0, start : start + TILE, :]
                        sin = turn_ref[index, 1, start : start + TILE, :]
                        real = halves(*reals)
                        if imags[0] is None and imags[1] is None:
                            put(index, start, real * cos)
                            put(index, inner + start, real * -sin)
                        else:
                            imag = halves(*imags)
                            put(index, start, real * cos + imag * sin)
                            put(index, inner + start, imag * cos - real * sin)


def expand(core, target):
    row = lax.broadcasted_iota(jnp.int32, (TILE, core.shape[1]), 0)
    same = row == lanes_of(row.shape) % TILE
    for index in range(OUTER):
        wide = jnp.broadcast_to(core[index : index + 1], row.shape)
        target[index * TILE : (index + 1) * TILE, :] = jnp.where(same, wide, 0.0).astype(jnp.bfloat16)


def turn_pair(turn_ref, start, count, bin_index, lanes):
    rows = pl.ds(start, count)
    cos = jnp.broadcast_to(turn_ref[rows, bin_index : bin_index + 1], (count, lanes))
    at = LANES // 2 + bin_index
    sin = jnp.broadcast_to(turn_ref[rows, at : at + 1], (count, lanes))
    return cos, sin


def store_sections(section, turn_ref, wide_ref, tile, lanes, put):
    start = tile * TILE
    by_row = section.reshape(OUTER, TILE, lanes)
    for bin_index in range(BINS):
        cos, sin = turn_pair(turn_ref, start, TILE, bin_index, lanes)
        wide_ref[bin_index, 0, start : start + TILE, :] = cos
        wide_ref[bin_index, 1, start : start + TILE, :] = sin
        if bin_index in (0, HALF):
            real = by_row[0 if bin_index == 0 else 1]
            put(bin_index, start, real * cos, real * -sin)
        else:
            real = by_row[2 * bin_index]
            imag = by_row[2 * bin_index + 1]
            put(bin_index, start, real * cos + imag * sin, imag * cos - real * sin)


def short_filter(value, taps, later, near=None):
    rows = value.shape[0]
    row = lax.broadcasted_iota(jnp.int32, (EXTRA, LANES), 0)
    shifted = []
    for lag in (1, 2):
        moved = pltpu.roll(value, rows - lag if later else lag, 0)
        shift = EXTRA - lag if later else lag
        fill = 0.0 if near is None else pltpu.roll(near, shift, 0)
        if later:
            tail = jnp.where(row < EXTRA - lag, moved[rows - EXTRA :], fill)
            moved = jnp.concatenate([moved[: rows - EXTRA], tail], axis=0)
        else:
            head = jnp.where(row >= lag, moved[:EXTRA], fill)
            moved = jnp.concatenate([head, moved[EXTRA:]], axis=0)
        shifted.append(moved)
    return taps[0:1] * value + taps[1:2] * shifted[0] + taps[2:3] * shifted[1]


def chunk_filter(ref, start, columns, taps, later):
    end = start + CHUNK
    value = ref[start:end, columns].astype(jnp.float32)
    near = None
    if later and end < ref.shape[0]:
        near = ref[end : end + TILE, columns].astype(jnp.float32)[:EXTRA]
    elif not later and start > 0:
        near = ref[start - TILE : start, columns].astype(jnp.float32)[EXTRA:]
    return short_filter(value, taps, later, near)


def gate_kernel(
    fwd_hbm, rev_hbm, tokens_hbm, taps_hbm, out_hbm, fwd_o_hbm, rev_o_hbm,
    fwd_ref, rev_ref, fwd_edge_ref, rev_edge_ref, tokens_ref, taps_ref, out_ref, fwd_o_ref, rev_o_ref,
    first_q_ref, sems, small_sems, out_sems
):
    rows = fwd_ref.shape[0]
    width = fwd_ref.shape[1] // 2
    lanes = out_ref.shape[2]
    count = lanes // 2
    small = [
        pltpu.make_async_copy(taps_hbm, taps_ref, small_sems.at[0]),
        pltpu.make_async_copy(tokens_hbm, tokens_ref, small_sems.at[1]),
        pltpu.make_async_copy(
            fwd_hbm.at[pl.ds(rows - TILE, TILE), pl.ds(2 * width, width)],
            fwd_edge_ref,
            small_sems.at[2],
        ),
        pltpu.make_async_copy(
            rev_hbm.at[pl.ds(0, TILE), pl.ds(2 * width, width)], rev_edge_ref, small_sems.at[3]
        ),
    ]
    loads, stores = [], []
    for step in range(rows // CHUNK):
        start, end = step * CHUNK, (step + 1) * CHUNK
        rev_start = start + TILE if step else 0
        rev_end = min(end + TILE, rows)
        part = (pl.ds(start, CHUNK), pl.ds(0, 2 * width))
        rev_part = (pl.ds(rev_start, rev_end - rev_start), pl.ds(0, 2 * width))
        copies = [
            pltpu.make_async_copy(fwd_hbm.at[part], fwd_ref.at[part], sems.at[step, 0]),
            pltpu.make_async_copy(rev_hbm.at[rev_part], rev_ref.at[rev_part], sems.at[step, 1]),
        ]
        for copy in copies:
            copy.start()
        loads.append(copies)
        if step == 0:
            for copy in small[:2]:
                copy.start()
    for copy in small[2:]:
        copy.start()
    for copy in small[:2]:
        copy.wait()
    known_row = jnp.where(tokens_ref[...] != 4, 1.0, 0.0).astype(jnp.float32)
    known = jnp.transpose(jnp.broadcast_to(known_row, (LANES, rows)))
    edge_row = lax.broadcasted_iota(jnp.int32, (EXTRA, LANES), 0)

    def piece_of(left, right, piece):
        left_shift = (LANES - piece * count) % LANES
        right_shift = (LANES + count - piece * count) % LANES
        left = pltpu.roll(left, left_shift, 1) if left_shift else left
        right = pltpu.roll(right, right_shift, 1) if right_shift else right
        return jnp.where(lanes_of(left.shape) < count, left, right)[:, :lanes].astype(jnp.bfloat16)

    def rows_of(ref, columns, start):
        return ref[start : start + TILE, columns].astype(jnp.float32)

    def with_rows(edge, rows_at, value, at):
        moved = pltpu.roll(value, (rows_at - at) % EXTRA, 0)
        return jnp.where((edge_row >= rows_at) & (edge_row < rows_at + 2), moved, edge)

    pieces = LANES // count
    for step in range(rows // CHUNK):
        start = step * CHUNK
        final = start + CHUNK == rows
        for copy in loads[step] + (small[2:] if final else []):
            copy.wait()
        here = slice(start, start + CHUNK)
        for block in range(width // LANES):
            low = block * LANES
            at_v = slice(low, low + LANES)
            at_q = slice(width + low, width + low + LANES)
            taps_v, taps_q = taps_ref[:, at_v], taps_ref[:, at_q]
            fwd_v = chunk_filter(fwd_ref, start, at_v, taps_v, False)
            fwd_q = chunk_filter(fwd_ref, start, at_q, taps_q, False)
            fwd_body = known[here] * fwd_q * fwd_v
            rev_v = chunk_filter(rev_ref, start, at_v, taps_v, True)
            rev_q = chunk_filter(rev_ref, start, at_q, taps_q, True)
            rev_body = known[here] * rev_q * rev_v
            if start == 0:
                part = jnp.where(known[:EXTRA] > 0.0, fwd_v[:EXTRA], jnp.inf)
                head = jnp.where(edge_row < 2, part, fwd_body[:EXTRA])
                fwd_body = jnp.concatenate([head, fwd_body[EXTRA:]], axis=0)
                first_q_ref[:, at_v] = fwd_q[:EXTRA]
            if final:
                part = jnp.where(known[rows - EXTRA :] > 0.0, rev_v[CHUNK - EXTRA :], jnp.inf)
                tail = jnp.where(edge_row >= EXTRA - 2, part, rev_body[CHUNK - EXTRA :])
                rev_body = jnp.concatenate([rev_body[: CHUNK - EXTRA], tail], axis=0)
                raw_o = rows_of(fwd_edge_ref, at_v, 0)[EXTRA:]
                edge = jnp.where(edge_row < 2, first_q_ref[:, at_v], raw_o)
                edge = with_rows(edge, 2, rows_of(fwd_ref, at_v, rows - TILE)[EXTRA:], 6)
                edge = with_rows(edge, 4, rows_of(fwd_ref, at_q, rows - TILE)[EXTRA:], 6)
                fwd_body = jnp.concatenate([fwd_body, edge], axis=0)
                place = (
                    slice(low // EDGE_LANES * EDGE_ROWS, (low // EDGE_LANES + 1) * EDGE_ROWS),
                    slice(low % EDGE_LANES, low % EDGE_LANES + LANES),
                )
                fwd_o_ref[place] = pltpu.roll(raw_o, 2, 0)[:EDGE_ROWS]
                raw_o = rows_of(rev_edge_ref, at_v, 0)[:EXTRA]
                edge = jnp.where(edge_row < 2, pltpu.roll(rev_q[CHUNK - EXTRA :], 2, 0), 0.0)
                edge = with_rows(edge, 2, rows_of(rev_ref, at_v, 0)[:EXTRA], 0)
                edge = with_rows(edge, 4, rows_of(rev_ref, at_q, 0)[:EXTRA], 0)
                rev_body = jnp.concatenate([rev_body, edge], axis=0)
                rev_o_ref[place] = raw_o[:EDGE_ROWS]
            for piece in range(pieces):
                out_ref[block * pieces + piece, start : start + fwd_body.shape[0], :] = piece_of(
                    fwd_body, rev_body, piece
                )
        part = (slice(None), pl.ds(start, CHUNK + (EXTRA if final else 0)))
        copy = pltpu.make_async_copy(out_ref.at[part], out_hbm.at[part], out_sems.at[step])
        copy.start()
        stores.append(copy)
    for at, (source, target) in enumerate(((fwd_o_ref, fwd_o_hbm), (rev_o_ref, rev_o_hbm))):
        copy = pltpu.make_async_copy(source, target, small_sems.at[4 + at])
        copy.start()
        stores.append(copy)
    for copy in stores:
        copy.wait()


def sections_kernel(
    me_ref, kernel_hbm, skip_hbm, taps_hbm, core_hbm, phase_hbm,
    high, low, own_taps_ref, core_ref, phase_ref,
    kernel_ref, skip_ref, taps_ref, wide_ref, enter_ref, turn_ref, signal, sems
):
    moves = (
        (phase_hbm, phase_ref), (kernel_hbm, kernel_ref), (skip_hbm, skip_ref),
        (taps_hbm, taps_ref), (core_hbm, wide_ref), (core_hbm.at[0], core_ref),
    )
    copies = [
        pltpu.make_async_copy(source, target, sems.at[at])
        for at, (source, target) in enumerate(moves)
    ]
    for copy in copies:
        copy.start()
    count, length = kernel_ref.shape
    lanes = 2 * count
    inner = length // HALF
    half_rows = signal.shape[2]
    rows = 2 * half_rows
    per = inner // rows
    width = taps_ref.shape[1] // 3

    copies[0].wait()
    for index in range(PAIRS):
        for part in range(2):
            columns = [part * (LANES // 2) + min(2 * index + b, BINS) for b in range(2)]
            sides = [
                jnp.broadcast_to(phase_ref[:, column : column + 1], (inner, lanes))
                for column in columns
            ]
            turn_ref[index, part] = jnp.where(lanes_of((inner, lanes)) < count, *sides)

    for copy in copies[1:5]:
        copy.wait()
    me = me_ref[0]
    per_block = LANES // count
    block = me // per_block
    shift = lax.rem(LANES - (me - block * per_block) * count, LANES)
    for which in range(2):
        column = pl.multiple_of(which * width + block * LANES, LANES)
        own = pltpu.roll(taps_ref[:, pl.ds(column, LANES)], shift, 1)
        both = jnp.where(lanes_of(own.shape) < count, own, pltpu.roll(own, count, 1))[:, :lanes]
        for tap in range(3):
            own_taps_ref[3 * which + tap : 3 * which + tap + 1, :] = both[tap : tap + 1]
    own_taps_ref[6:8, :] = jnp.zeros((2, lanes), jnp.float32)

    for start in range(0, length, rows):
        piece = kernel_ref[:, start : start + rows]
        both = jnp.concatenate([piece, pltpu.roll(piece, half_rows, 1)], axis=0)
        turned = jnp.transpose(both)[:half_rows]
        if start == 0:
            gain = skip_ref[...]
            gains = jnp.concatenate([gain, jnp.zeros_like(gain)], axis=1)
            row = lax.broadcasted_iota(jnp.int32, turned.shape, 0)
            turned = turned + jnp.where(row == 0, gains, 0.0)
        signal[start // inner, start % inner // rows] = turned

    def load(group, tile):
        return signal[:, group, tile * TILE : (tile + 1) * TILE, :].reshape(HALF * TILE, lanes)

    def enter_dots(value):
        top = value.astype(jnp.bfloat16)
        rest = (value - top.astype(jnp.float32)).astype(jnp.bfloat16)
        return table_dot(enter_ref, top) + dot(enter_ref[0], rest)

    def put(index, start, value):
        top = value.astype(jnp.bfloat16)
        high[index, start : start + TILE, :] = top
        low[index, start : start + TILE, :] = (value - top.astype(jnp.float32)).astype(jnp.bfloat16)

    for part in range(2):
        expand(wide_ref[part], enter_ref.at[part])
    enter_stage(load, enter_dots, turn_ref, per, half_rows, put)
    copies[5].wait()


def spectrum_kernel(high, low, mix_hbm, *refs):
    *spec_refs, mix_out_ref, mix_ref, sems = refs
    copies = [
        pltpu.make_async_copy(mix_hbm, mix_ref, sems.at[0]),
        pltpu.make_async_copy(mix_hbm.at[0], mix_out_ref, sems.at[1]),
    ]
    for copy in copies:
        copy.start()
    for copy in copies:
        copy.wait()
    inner = high.shape[1] // 2
    lanes = high.shape[2]
    count = lanes // 2
    length = inner * HALF
    for first in range(0, PAIRS, 2):
        group = range(first, min(first + 2, PAIRS))
        top = jnp.concatenate([high[index] for index in group], axis=1)
        rest = jnp.concatenate([low[index] for index in group], axis=1)
        spec = table_dot(mix_ref, top) + dot(mix_ref[0], rest)
        for at, index in enumerate(group):
            pair = spec[:, at * lanes : (at + 1) * lanes]
            left = lanes_of((inner, lanes)) < count
            for side in range(2):
                if 2 * index + side == BINS:
                    break
                for part in range(2):
                    here = pair[part * inner : (part + 1) * inner]
                    there = swap(here)
                    value = jnp.where(left, there, here) if side else jnp.where(left, here, there)
                    if part:
                        value = jnp.where(left, value, -value)
                    weight = (1.0 if 2 * index + side in (0, HALF) else 2.0) / (2 * length)
                    value = value * weight
                    which, place = divmod(2 * index + side, BIN_GROUP)
                    spec_refs[which][place, part * inner : (part + 1) * inner, :] = value


def mended_tiles(recv_ref, own_taps_ref, group, rows):
    blocks, per, _, lanes = recv_ref.shape
    count = lanes // 2
    taps = own_taps_ref[...]
    edge = recv_ref[:, group, rows : rows + EXTRA, :].astype(jnp.float32)
    blank = jnp.zeros((1, EXTRA, lanes), jnp.float32)
    if group > 0:
        before = recv_ref[:, group - 1, rows : rows + EXTRA, :].astype(jnp.float32)
    else:
        shifted = recv_ref[: blocks - 1, per - 1, rows : rows + EXTRA, :].astype(jnp.float32)
        before = jnp.concatenate([blank, shifted], axis=0)
    if group < per - 1:
        after = recv_ref[:, group + 1, rows : rows + EXTRA, :].astype(jnp.float32)
    else:
        shifted = recv_ref[1:, 0, rows : rows + EXTRA, :].astype(jnp.float32)
        after = jnp.concatenate([shifted, blank], axis=0)
    row = lax.broadcasted_iota(jnp.int32, (EXTRA, lanes), 0)
    lane = lax.broadcasted_iota(jnp.int32, (EXTRA, lanes), 1)
    first, last = [], []
    for block in range(blocks):
        top = recv_ref[block, group, :TILE, :].astype(jnp.float32)
        part = top[:EXTRA]
        near = before[block]
        mix_v = part + taps[2:3] * pltpu.roll(near, 6, 0)
        mix_v = mix_v + jnp.where(row == 0, taps[1:2] * pltpu.roll(near, 5, 0), 0.0)
        mix_q = edge[block] + taps[5:6] * pltpu.roll(near, 4, 0)
        mix_q = mix_q + jnp.where(row == 0, taps[4:5] * pltpu.roll(near, 3, 0), 0.0)
        fixed = jnp.where(part == jnp.inf, 0.0, mix_q * mix_v)
        fixed = jnp.where((row < 2) & (lane < count), fixed, part)
        first.append(jnp.concatenate([fixed, top[EXTRA:]], axis=0).astype(jnp.bfloat16))

        end = recv_ref[block, group, rows - TILE : rows, :].astype(jnp.float32)
        part = end[EXTRA:]
        near = after[block]
        mix_v = part + taps[2:3] * pltpu.roll(near, 4, 0)
        mix_v = mix_v + jnp.where(row == 7, taps[1:2] * pltpu.roll(near, 5, 0), 0.0)
        mix_q = pltpu.roll(edge[block], 6, 0) + taps[5:6] * pltpu.roll(near, 2, 0)
        mix_q = mix_q + jnp.where(row == 7, taps[4:5] * pltpu.roll(near, 3, 0), 0.0)
        fixed = jnp.where(part == jnp.inf, 0.0, mix_q * mix_v)
        fixed = jnp.where((row >= 6) & (lane >= count), fixed, part)
        last.append(jnp.concatenate([end[:EXTRA], fixed], axis=0).astype(jnp.bfloat16))
    return jnp.stack(first), jnp.stack(last)


def filter_kernel(recv_ref, own_taps_ref, core_ref, turn_ref, *refs):
    *spec_refs, mix_ref, out_ref, sections, returned, enter_ref, wide_ref = refs
    expand(core_ref[...], enter_ref)
    blocks, per, padded, lanes = recv_ref.shape
    rows = padded - EXTRA
    inner = per * rows
    tiles = rows // TILE

    def put(bin_index, start, real, imag):
        sections[bin_index, start : start + TILE, :] = real.astype(jnp.bfloat16)
        sections[bin_index, inner + start : inner + start + TILE, :] = imag.astype(jnp.bfloat16)

    for group in range(per):
        first, last = mended_tiles(recv_ref, own_taps_ref, group, rows)
        loaded = [first]
        for tile in range(1, tiles - 1):
            loaded.append(recv_ref[:, group, tile * TILE : (tile + 1) * TILE, :])
        loaded.append(last)
        loaded = [value.reshape(blocks * TILE, lanes) for value in loaded]
        def section_of(tile):
            return dot(enter_ref[...], jnp.concatenate(loaded[tile : tile + 2], axis=1))

        order = list(range(2, tiles - 2, 2)) + [0, tiles - 2]
        ahead = section_of(order[0])
        for place, tile in enumerate(order):
            section = ahead
            if place + 1 < len(order):
                ahead = section_of(order[place + 1])
            at = group * tiles + tile
            store_sections(section[:, :lanes], turn_ref, wide_ref, at, lanes, put)
            store_sections(section[:, lanes:], turn_ref, wide_ref, at + 1, lanes, put)

    def bins_from(first):
        return range(first, min(first + 2, BINS))

    def spec_of(first):
        pair = [sections[b] for b in bins_from(first)]
        return dot(mix_ref[...], jnp.concatenate(pair, axis=1))

    def back_of(first, spec):
        gains = [spec_refs[b // BIN_GROUP][b % BIN_GROUP] for b in bins_from(first)]
        gain = jnp.concatenate(gains, axis=1)
        real, imag = spec[:inner], spec[inner:]
        gain_real, gain_imag = gain[:inner], gain[inner:]
        product = jnp.concatenate(
            [real * gain_real - imag * gain_imag, -real * gain_imag - imag * gain_real], axis=0
        ).astype(jnp.bfloat16)
        return dot(mix_ref[...], product)

    def store_returned(first, back):
        for at, b in enumerate(bins_from(first)):
            real = back[:inner, at * lanes : (at + 1) * lanes]
            imag = back[inner:, at * lanes : (at + 1) * lanes]
            cos, sin = wide_ref[b, 0], wide_ref[b, 1]
            returned[slot(b, 0)] = (real * cos + imag * sin).astype(jnp.bfloat16)
            if b not in (0, HALF):
                returned[slot(b, 1)] = (real * sin - imag * cos).astype(jnp.bfloat16)

    ahead, behind = spec_of(0), None
    for first in range(0, BINS, 2):
        spec = ahead
        if first + 2 < BINS:
            ahead = spec_of(first + 2)
        back = back_of(first, spec)
        if behind is not None:
            store_returned(first - 2, behind)
        behind = back
    store_returned(BINS - 1, behind)

    leave = jnp.transpose(enter_ref[...])
    for tile in range(0, inner // TILE, 2):
        pair = jnp.concatenate(
            [
                returned[:, at * TILE : (at + 1) * TILE, :].reshape(OUTER * TILE, lanes)
                for at in (tile, tile + 1)
            ],
            axis=1,
        )
        value = dot(leave, pair).astype(jnp.bfloat16)
        group, place = divmod(tile, tiles)
        for at in (0, 1):
            start = (place + at) * TILE
            out_ref[:, group, start : start + TILE, :] = value[
                :, at * lanes : (at + 1) * lanes
            ].reshape(blocks, TILE, lanes)


def mixing_kernel(
    ret_ref, fwd_o_ref, rev_o_ref, fwd_ref, rev_ref, taps_ref, weight_ref, out_ref, combined, total
):
    rows = fwd_ref.shape[0]
    width = weight_ref.shape[0]
    count = ret_ref.shape[2] // 2
    pieces = LANES // count
    blocks = width // LANES
    edge_row = lax.broadcasted_iota(jnp.int32, (EXTRA, LANES), 0)
    mirror = LANES - 1 - lax.broadcasted_iota(jnp.int32, (rows, LANES), 1)

    def near_edge(edges, block, target):
        low = block * LANES
        at_row = low // EDGE_LANES * EDGE_ROWS
        start = at_row // EXTRA * EXTRA
        at_lane = low % EDGE_LANES
        tile = edges[start : start + EXTRA, at_lane : at_lane + LANES]
        shift = (target - at_row + start) % EXTRA
        return pltpu.roll(tile, shift, 0) if shift else tile

    def columns(block, which):
        chunks = [
            ret_ref[block * pieces + piece].astype(jnp.float32)[
                :, which * count : (which + 1) * count
            ]
            for piece in range(pieces)
        ]
        return jnp.concatenate(chunks, axis=1)

    for block in range(blocks):
        low = 2 * width + block * LANES
        taps = taps_ref[:, low : low + LANES]
        mixed = short_filter(fwd_ref[:, low : low + LANES].astype(jnp.float32), taps, False)
        more = jnp.where(edge_row < 2, taps[2:3] * near_edge(fwd_o_ref, block, 0), 0.0)
        last = jnp.where(edge_row == 0, taps[1:2] * near_edge(fwd_o_ref, block, -1), 0.0)
        mixed = jnp.concatenate([mixed[:EXTRA] + more + last, mixed[EXTRA:]], axis=0)
        gated = mixed * columns(block, 0)

        other = blocks - 1 - block
        low = 2 * width + other * LANES
        taps = taps_ref[:, low : low + LANES]
        mixed = short_filter(rev_ref[:, low : low + LANES].astype(jnp.float32), taps, True)
        more = jnp.where(edge_row >= 6, taps[2:3] * near_edge(rev_o_ref, other, 6), 0.0)
        first = jnp.where(edge_row == 7, taps[1:2] * near_edge(rev_o_ref, other, 7), 0.0)
        tail = mixed[rows - EXTRA :] + more + first
        mixed = jnp.concatenate([mixed[: rows - EXTRA], tail], axis=0)
        turned = jnp.take_along_axis(mixed * columns(other, 1), mirror, axis=1)
        combined[:, block * LANES : (block + 1) * LANES] = (gated + turned).astype(jnp.bfloat16)
        if block % 2:
            part = slice((block - 1) * LANES, (block + 1) * LANES)
            product = dot(combined[:, part], weight_ref[part, :])
            if block == 1:
                total[...] = product
            elif block < blocks - 1:
                total[...] += product
            else:
                out_ref[...] = (total[...] + product).astype(jnp.bfloat16)


HBM = pl.BlockSpec(memory_space=pltpu.HBM)
VMEM = pl.BlockSpec(memory_space=pltpu.VMEM)
SMEM = pl.BlockSpec(memory_space=pltpu.SMEM)


def params(limit=VMEM_BYTES):
    return pltpu.CompilerParams(vmem_limit_bytes=limit)


def cost(flops, size):
    return pl.CostEstimate(flops=flops, bytes_accessed=size, transcendentals=0)


def exchange(value):
    return lax.all_to_all(value, "ctx", split_axis=0, concat_axis=0, tiled=True)


def shifted(value, steps):
    count = lax.axis_size("ctx")
    first, end = max(0, -steps), min(count, count - steps)
    return lax.ppermute(value, "ctx", [(source, source + steps) for source in range(first, end)])


def per_device(fwd_proj, rev_proj, tokens, short_taps, long_kernel, skip_gain, out_weight):
    rows = fwd_proj.shape[0]
    half_rows = rows // 2
    width = fwd_proj.shape[1] // 3
    count, length = long_kernel.shape
    devices = length // rows
    lanes = 2 * count
    inner = length // HALF
    per = devices // HALF
    padded = rows + EXTRA
    edge_block = (EDGE_ROWS * width // EDGE_LANES, EDGE_LANES)
    tables = [jnp.asarray(table) for table in dft_tables(length)]
    core, mix, phases = tables
    outer_shape = (OUTER * TILE, HALF * TILE)
    block = (devices, padded, lanes)

    sent, fwd_o, rev_o = pl.pallas_call(
        gate_kernel,
        out_shape=(
            jax.ShapeDtypeStruct(block, jnp.bfloat16),
            jax.ShapeDtypeStruct(edge_block, jnp.float32),
            jax.ShapeDtypeStruct(edge_block, jnp.float32),
        ),
        in_specs=[HBM] * 4,
        out_specs=(HBM,) * 3,
        scratch_shapes=[
            pltpu.VMEM((rows, 2 * width), jnp.bfloat16),
            pltpu.VMEM((rows, 2 * width), jnp.bfloat16),
            pltpu.VMEM((TILE, width), jnp.bfloat16),
            pltpu.VMEM((TILE, width), jnp.bfloat16),
            pltpu.VMEM((1, rows), jnp.int32),
            pltpu.VMEM(short_taps.shape, jnp.float32),
            pltpu.VMEM(block, jnp.bfloat16),
            pltpu.VMEM(edge_block, jnp.float32),
            pltpu.VMEM(edge_block, jnp.float32),
            pltpu.VMEM((EXTRA, width), jnp.float32),
            pltpu.SemaphoreType.DMA((rows // CHUNK, 2)),
            pltpu.SemaphoreType.DMA((6,)),
            pltpu.SemaphoreType.DMA((rows // CHUNK,)),
        ],
        compiler_params=params(FULL_VMEM_BYTES),
        name="gate",
    )(fwd_proj, rev_proj, tokens.reshape(1, rows), short_taps)


    me = lax.axis_index("ctx").astype(jnp.int32).reshape(1)
    sent, me = lax.optimization_barrier((sent, me))
    received = exchange(sent)
    section_shape = jax.ShapeDtypeStruct((PAIRS, 2 * inner, lanes), jnp.bfloat16)
    spectrum_cost = cost(3 * PAIRS * 2 * (2 * inner) ** 2 * lanes, 4 * 1024 * 1024)
    high, low, own_taps, own_core, own_phases = pl.pallas_call(
        sections_kernel,
        out_shape=(
            section_shape,
            section_shape,
            jax.ShapeDtypeStruct((8, lanes), jnp.float32),
            jax.ShapeDtypeStruct(core.shape[1:], jnp.float32),
            jax.ShapeDtypeStruct(phases.shape, jnp.float32),
        ),
        in_specs=[SMEM] + [HBM] * 5,
        out_specs=(VMEM,) * 5,
        scratch_shapes=[
            pltpu.VMEM((count, length), jnp.float32),
            pltpu.VMEM((1, count), jnp.float32),
            pltpu.VMEM(short_taps.shape, jnp.float32),
            pltpu.VMEM(core.shape, jnp.float32),
            pltpu.VMEM((2,) + outer_shape, jnp.bfloat16),
            pltpu.VMEM((PAIRS, 2, inner, lanes), jnp.float32),
            pltpu.VMEM((HALF, per, half_rows, lanes), jnp.float32),
            pltpu.SemaphoreType.DMA((6,)),
        ],
        compiler_params=params(),
        cost_estimate=spectrum_cost,
        name="sections",
    )(me, long_kernel, skip_gain.reshape(1, count), short_taps, core, phases)

    own_taps, fwd_o, rev_o = lax.optimization_barrier((own_taps, fwd_o, rev_o))
    fwd_o = shifted(fwd_o, 1)
    rev_o = shifted(rev_o, -1)
    own_taps, fwd_o, rev_o = lax.optimization_barrier((own_taps, fwd_o, rev_o))

    groups = [min(BIN_GROUP, BINS - first) for first in range(0, BINS, BIN_GROUP)]
    spectrum = pl.pallas_call(
        spectrum_kernel,
        out_shape=tuple(
            jax.ShapeDtypeStruct((group, 2 * inner, lanes), jnp.float32) for group in groups
        )
        + (jax.ShapeDtypeStruct(mix.shape[1:], jnp.bfloat16),),
        in_specs=[VMEM, VMEM, HBM],
        out_specs=(VMEM,) * (len(groups) + 1),
        scratch_shapes=[
            pltpu.VMEM(mix.shape, jnp.bfloat16),
            pltpu.SemaphoreType.DMA((2,)),
        ],
        compiler_params=params(),
        cost_estimate=spectrum_cost,
        name="spectrum",
    )(high, low, mix)

    filtered = pl.pallas_call(
        filter_kernel,
        out_shape=jax.ShapeDtypeStruct((HALF, per, rows, lanes), jnp.bfloat16),
        in_specs=[VMEM] * (4 + len(spectrum)),
        out_specs=VMEM,
        scratch_shapes=[
            pltpu.VMEM((BINS, 2 * inner, lanes), jnp.bfloat16),
            pltpu.VMEM((OUTER, inner, lanes), jnp.bfloat16),
            pltpu.VMEM(outer_shape, jnp.bfloat16),
            pltpu.VMEM((BINS, 2, inner, lanes), jnp.float32),
        ],
        compiler_params=params(),
        cost_estimate=cost(4 * PAIRS * 4 * (2 * inner) ** 2 * lanes, 4 * 1024 * 1024),
        name="filter",
    )(received.reshape(HALF, per, padded, lanes), own_taps, own_core, own_phases, *spectrum)

    returned = exchange(filtered.reshape(devices, rows, lanes))

    return pl.pallas_call(
        mixing_kernel,
        out_shape=jax.ShapeDtypeStruct((rows, width), jnp.bfloat16),
        in_specs=[VMEM] * 7,
        out_specs=VMEM,
        scratch_shapes=[
            pltpu.VMEM((rows, width), jnp.bfloat16),
            pltpu.VMEM((rows, width), jnp.float32),
        ],
        compiler_params=params(),
        cost_estimate=cost(2 * rows * width * width, 4 * 1024 * 1024),
        name="mixing",
    )(returned, fwd_o, rev_o, fwd_proj, rev_proj, short_taps, out_weight)


def solution(mesh):
    in_specs = (
        P(("dp", "ctx"), None),
        P(("dp", "ctx"), None),
        P(("dp", "ctx")),
        P(),
        P("ctx", None),
        P("ctx"),
        P(),
    )
    out_specs = P(("dp", "ctx"), None)
    return jax.shard_map(
        per_device, mesh=mesh, in_specs=in_specs, out_specs=out_specs, check_vma=False
    )
```

```python
import functools

import jax
import jax.numpy as jnp
import ml_dtypes
import numpy as np
from jax import lax
from jax.experimental import pallas as pl
from jax.experimental.pallas import tpu as pltpu
from jax.sharding import PartitionSpec as P

OUTER = 32
HALF = OUTER // 2
BINS = HALF + 1
PAIRS = (BINS + 1) // 2
EXTRA = 8
LANES = 128
TILE = 16
CHUNK = 64
BIN_GROUP = 2
VMEM_BYTES = 30 * 1024 * 1024
EDGE_LANES = 256
EDGE_ROWS = 2
FULL_VMEM_BYTES = 60000000


def split_table(table):
    high = table.astype(np.float32).astype(ml_dtypes.bfloat16)
    low = (table - high.astype(np.float64)).astype(np.float32).astype(ml_dtypes.bfloat16)
    return np.stack([high, low])


def outer_rows():
    rows = [(0, 0), (HALF, 0)]
    for bin_index in range(1, HALF):
        rows += [(bin_index, 0), (bin_index, 1)]
    return rows


def dft_tables(length):
    inner = length // HALF
    total = 2 * length
    blocks = np.arange(HALF)
    enter = np.zeros((OUTER, HALF))
    for row, (bin_index, part) in enumerate(outer_rows()):
        phase = 2.0 * np.pi * (bin_index * blocks % OUTER) / OUTER
        enter[row] = -np.sin(phase) if part else np.cos(phase)
    angles = 2.0 * np.pi * (np.outer(np.arange(inner), np.arange(inner)) % inner) / inner
    cos, sin = np.cos(angles), np.sin(angles)
    mix = np.block([[cos, sin], [-sin, cos]])
    turn = np.zeros((inner, LANES))
    turn_phase = 2.0 * np.pi * np.outer(np.arange(inner), np.arange(BINS)) / total
    turn[:, :BINS] = np.cos(turn_phase)
    turn[:, LANES // 2 : LANES // 2 + BINS] = np.sin(turn_phase)
    core = np.repeat(split_table(enter).astype(np.float32), TILE, axis=2)
    return (
        core,
        split_table(mix),
        turn.astype(np.float32),
    )


def dot(left, right):
    return jnp.dot(left, right, preferred_element_type=jnp.float32)


def table_dot(table_ref, right):
    return dot(table_ref[0], right) + dot(table_ref[1], right)


def lanes_of(shape):
    return lax.broadcasted_iota(jnp.int32, shape, len(shape) - 1)


def swap(value):
    lanes = value.shape[1]
    if lanes == LANES:
        return pltpu.roll(value, lanes // 2, 1)
    return jnp.concatenate([value[:, lanes // 2 :], value[:, : lanes // 2]], axis=1)


def trade(one, two):
    left = lanes_of(one.shape) < one.shape[1] // 2
    middle = swap(jnp.where(left, two, one))
    return jnp.where(left, one, middle), jnp.where(left, middle, two)


def left_halves(one, two):
    value = one if one is not None else two
    left = lanes_of(value.shape) < value.shape[1] // 2
    one = jnp.zeros_like(value) if one is None else one
    two = jnp.zeros_like(value) if two is None else swap(two)
    return jnp.where(left, one, two)


def right_halves(one, two):
    value = one if one is not None else two
    left = lanes_of(value.shape) < value.shape[1] // 2
    one = jnp.zeros_like(value) if one is None else swap(one)
    two = jnp.zeros_like(value) if two is None else two
    return jnp.where(left, one, two)


def slot(bin_index, part):
    if bin_index >= BINS or (part and bin_index in (0, HALF)):
        return None
    if bin_index in (0, HALF):
        return bin_index // HALF
    return 2 * bin_index + part


def enter_stage(load, dots, turn_ref, per, half_rows, put):
    inner = 2 * per * half_rows
    for group in range(per):
        for tile in range(0, half_rows // TILE, 2):
            pair = [load(group, tile), load(group, tile + 1)]
            lanes = pair[0].shape[1]
            section = dots(jnp.concatenate(pair, axis=1))
            for which in range(2):
                by_row = section[:, which * lanes : (which + 1) * lanes].reshape(OUTER, TILE, lanes)

                def part_of(bin_index, part):
                    row = slot(bin_index, part)
                    return None if row is None else by_row[row]

                for index in range(PAIRS):
                    bins = (2 * index, 2 * index + 1)
                    reals = [part_of(b, 0) for b in bins]
                    imags = [part_of(b, 1) for b in bins]
                    for side, halves in enumerate((left_halves, right_halves)):
                        start = (2 * group + side) * half_rows + (tile + which) * TILE
                        cos = turn_ref[index, 0, start : start + TILE, :]
                        sin = turn_ref[index, 1, start : start + TILE, :]
                        real = halves(*reals)
                        if imags[0] is None and imags[1] is None:
                            put(index, start, real * cos)
                            put(index, inner + start, real * -sin)
                        else:
                            imag = halves(*imags)
                            put(index, start, real * cos + imag * sin)
                            put(index, inner + start, imag * cos - real * sin)


def expand(core, target):
    row = lax.broadcasted_iota(jnp.int32, (TILE, core.shape[1]), 0)
    same = row == lanes_of(row.shape) % TILE
    for index in range(OUTER):
        wide = jnp.broadcast_to(core[index : index + 1], row.shape)
        target[index * TILE : (index + 1) * TILE, :] = jnp.where(same, wide, 0.0).astype(jnp.bfloat16)


def turn_pair(turn_ref, start, count, bin_index, lanes):
    rows = pl.ds(start, count)
    cos = jnp.broadcast_to(turn_ref[rows, bin_index : bin_index + 1], (count, lanes))
    at = LANES // 2 + bin_index
    sin = jnp.broadcast_to(turn_ref[rows, at : at + 1], (count, lanes))
    return cos, sin


def store_sections(section, turn_ref, wide_ref, tile, lanes, put):
    start = tile * TILE
    by_row = section.reshape(OUTER, TILE, lanes)
    for bin_index in range(BINS):
        cos, sin = turn_pair(turn_ref, start, TILE, bin_index, lanes)
        wide_ref[bin_index, 0, start : start + TILE, :] = cos
        wide_ref[bin_index, 1, start : start + TILE, :] = sin
        if bin_index in (0, HALF):
            real = by_row[0 if bin_index == 0 else 1]
            put(bin_index, start, real * cos, real * -sin)
        else:
            real = by_row[2 * bin_index]
            imag = by_row[2 * bin_index + 1]
            put(bin_index, start, real * cos + imag * sin, imag * cos - real * sin)


def short_filter(value, taps, later, near=None):
    rows = value.shape[0]
    row = lax.broadcasted_iota(jnp.int32, (EXTRA, LANES), 0)
    shifted = []
    for lag in (1, 2):
        moved = pltpu.roll(value, rows - lag if later else lag, 0)
        shift = EXTRA - lag if later else lag
        fill = 0.0 if near is None else pltpu.roll(near, shift, 0)
        if later:
            tail = jnp.where(row < EXTRA - lag, moved[rows - EXTRA :], fill)
            moved = jnp.concatenate([moved[: rows - EXTRA], tail], axis=0)
        else:
            head = jnp.where(row >= lag, moved[:EXTRA], fill)
            moved = jnp.concatenate([head, moved[EXTRA:]], axis=0)
        shifted.append(moved)
    return taps[0:1] * value + taps[1:2] * shifted[0] + taps[2:3] * shifted[1]


def chunk_filter(ref, start, columns, taps, later):
    end = start + CHUNK
    value = ref[start:end, columns].astype(jnp.float32)
    near = None
    if later and end < ref.shape[0]:
        near = ref[end : end + TILE, columns].astype(jnp.float32)[:EXTRA]
    elif not later and start > 0:
        near = ref[start - TILE : start, columns].astype(jnp.float32)[EXTRA:]
    return short_filter(value, taps, later, near)


def gate_kernel(
    fwd_hbm, rev_hbm, tokens_hbm, taps_hbm, out_hbm, fwd_o_hbm, rev_o_hbm,
    fwd_ref, rev_ref, fwd_edge_ref, rev_edge_ref, tokens_ref, taps_ref, out_ref, fwd_o_ref, rev_o_ref,
    first_q_ref, sems, small_sems, out_sems
):
    rows = fwd_ref.shape[0]
    width = fwd_ref.shape[1] // 2
    lanes = out_ref.shape[2]
    count = lanes // 2
    small = [
        pltpu.make_async_copy(taps_hbm, taps_ref, small_sems.at[0]),
        pltpu.make_async_copy(tokens_hbm, tokens_ref, small_sems.at[1]),
        pltpu.make_async_copy(
            fwd_hbm.at[pl.ds(rows - TILE, TILE), pl.ds(2 * width, width)],
            fwd_edge_ref,
            small_sems.at[2],
        ),
        pltpu.make_async_copy(
            rev_hbm.at[pl.ds(0, TILE), pl.ds(2 * width, width)], rev_edge_ref, small_sems.at[3]
        ),
    ]
    loads, stores = [], []
    for step in range(rows // CHUNK):
        start, end = step * CHUNK, (step + 1) * CHUNK
        rev_start = start + TILE if step else 0
        rev_end = min(end + TILE, rows)
        part = (pl.ds(start, CHUNK), pl.ds(0, 2 * width))
        rev_part = (pl.ds(rev_start, rev_end - rev_start), pl.ds(0, 2 * width))
        copies = [
            pltpu.make_async_copy(fwd_hbm.at[part], fwd_ref.at[part], sems.at[step, 0]),
            pltpu.make_async_copy(rev_hbm.at[rev_part], rev_ref.at[rev_part], sems.at[step, 1]),
        ]
        for copy in copies:
            copy.start()
        loads.append(copies)
        if step == 0:
            for copy in small[:2]:
                copy.start()
    for copy in small[2:]:
        copy.start()
    for copy in small[:2]:
        copy.wait()
    known_row = jnp.where(tokens_ref[...] != 4, 1.0, 0.0).astype(jnp.float32)
    known = jnp.transpose(jnp.broadcast_to(known_row, (LANES, rows)))
    edge_row = lax.broadcasted_iota(jnp.int32, (EXTRA, LANES), 0)

    def piece_of(left, right, piece):
        left_shift = (LANES - piece * count) % LANES
        right_shift = (LANES + count - piece * count) % LANES
        left = pltpu.roll(left, left_shift, 1) if left_shift else left
        right = pltpu.roll(right, right_shift, 1) if right_shift else right
        return jnp.where(lanes_of(left.shape) < count, left, right)[:, :lanes].astype(jnp.bfloat16)

    def pieces_of(left, right):
        if pieces != 2:
            return [piece_of(left, right, piece) for piece in range(pieces)]
        return [value.astype(jnp.bfloat16) for value in trade(left, right)]

    def rows_of(ref, columns, start):
        return ref[start : start + TILE, columns].astype(jnp.float32)

    def with_rows(edge, rows_at, value, at):
        moved = pltpu.roll(value, (rows_at - at) % EXTRA, 0)
        return jnp.where((edge_row >= rows_at) & (edge_row < rows_at + 2), moved, edge)

    pieces = LANES // count
    for step in range(rows // CHUNK):
        start = step * CHUNK
        final = start + CHUNK == rows
        for copy in loads[step] + (small[2:] if final else []):
            copy.wait()
        here = slice(start, start + CHUNK)
        for block in range(width // LANES):
            low = block * LANES
            at_v = slice(low, low + LANES)
            at_q = slice(width + low, width + low + LANES)
            taps_v, taps_q = taps_ref[:, at_v], taps_ref[:, at_q]
            fwd_v = chunk_filter(fwd_ref, start, at_v, taps_v, False)
            fwd_q = chunk_filter(fwd_ref, start, at_q, taps_q, False)
            fwd_body = known[here] * fwd_q * fwd_v
            rev_v = chunk_filter(rev_ref, start, at_v, taps_v, True)
            rev_q = chunk_filter(rev_ref, start, at_q, taps_q, True)
            rev_body = known[here] * rev_q * rev_v
            if start == 0:
                part = jnp.where(known[:EXTRA] > 0.0, fwd_v[:EXTRA], jnp.inf)
                head = jnp.where(edge_row < 2, part, fwd_body[:EXTRA])
                fwd_body = jnp.concatenate([head, fwd_body[EXTRA:]], axis=0)
                first_q_ref[:, at_v] = fwd_q[:EXTRA]
            if final:
                part = jnp.where(known[rows - EXTRA :] > 0.0, rev_v[CHUNK - EXTRA :], jnp.inf)
                tail = jnp.where(edge_row >= EXTRA - 2, part, rev_body[CHUNK - EXTRA :])
                rev_body = jnp.concatenate([rev_body[: CHUNK - EXTRA], tail], axis=0)
                raw_o = rows_of(fwd_edge_ref, at_v, 0)[EXTRA:]
                edge = jnp.where(edge_row < 2, first_q_ref[:, at_v], raw_o)
                edge = with_rows(edge, 2, rows_of(fwd_ref, at_v, rows - TILE)[EXTRA:], 6)
                edge = with_rows(edge, 4, rows_of(fwd_ref, at_q, rows - TILE)[EXTRA:], 6)
                fwd_body = jnp.concatenate([fwd_body, edge], axis=0)
                place = (
                    slice(low // EDGE_LANES * EDGE_ROWS, (low // EDGE_LANES + 1) * EDGE_ROWS),
                    slice(low % EDGE_LANES, low % EDGE_LANES + LANES),
                )
                fwd_o_ref[place] = pltpu.roll(raw_o, 2, 0)[:EDGE_ROWS]
                raw_o = rows_of(rev_edge_ref, at_v, 0)[:EXTRA]
                edge = jnp.where(edge_row < 2, pltpu.roll(rev_q[CHUNK - EXTRA :], 2, 0), 0.0)
                edge = with_rows(edge, 2, rows_of(rev_ref, at_v, 0)[:EXTRA], 0)
                edge = with_rows(edge, 4, rows_of(rev_ref, at_q, 0)[:EXTRA], 0)
                rev_body = jnp.concatenate([rev_body, edge], axis=0)
                rev_o_ref[place] = raw_o[:EDGE_ROWS]
            for piece, value in enumerate(pieces_of(fwd_body, rev_body)):
                out_ref[block * pieces + piece, start : start + value.shape[0], :] = value
        part = (slice(None), pl.ds(start, CHUNK + (EXTRA if final else 0)))
        copy = pltpu.make_async_copy(out_ref.at[part], out_hbm.at[part], out_sems.at[step])
        copy.start()
        stores.append(copy)
    for at, (source, target) in enumerate(((fwd_o_ref, fwd_o_hbm), (rev_o_ref, rev_o_hbm))):
        copy = pltpu.make_async_copy(source, target, small_sems.at[4 + at])
        copy.start()
        stores.append(copy)
    for copy in stores:
        copy.wait()


def sections_kernel(
    me_ref, kernel_hbm, skip_hbm, taps_hbm, core_hbm, phase_hbm,
    high, low, own_taps_ref, core_ref, phase_ref,
    kernel_ref, skip_ref, taps_ref, wide_ref, enter_ref, turn_ref, signal, sems
):
    moves = (
        (phase_hbm, phase_ref), (kernel_hbm, kernel_ref), (skip_hbm, skip_ref),
        (taps_hbm, taps_ref), (core_hbm, wide_ref), (core_hbm.at[0], core_ref),
    )
    copies = [
        pltpu.make_async_copy(source, target, sems.at[at])
        for at, (source, target) in enumerate(moves)
    ]
    for copy in copies:
        copy.start()
    count, length = kernel_ref.shape
    lanes = 2 * count
    inner = length // HALF
    half_rows = signal.shape[2]
    rows = 2 * half_rows
    per = inner // rows
    width = taps_ref.shape[1] // 3

    copies[0].wait()
    for index in range(PAIRS):
        for part in range(2):
            columns = [part * (LANES // 2) + min(2 * index + b, BINS) for b in range(2)]
            sides = [
                jnp.broadcast_to(phase_ref[:, column : column + 1], (inner, lanes))
                for column in columns
            ]
            turn_ref[index, part] = jnp.where(lanes_of((inner, lanes)) < count, *sides)

    for copy in copies[1:5]:
        copy.wait()
    me = me_ref[0]
    per_block = LANES // count
    block = me // per_block
    shift = lax.rem(LANES - (me - block * per_block) * count, LANES)
    for which in range(2):
        column = pl.multiple_of(which * width + block * LANES, LANES)
        own = pltpu.roll(taps_ref[:, pl.ds(column, LANES)], shift, 1)
        both = jnp.where(lanes_of(own.shape) < count, own, pltpu.roll(own, count, 1))[:, :lanes]
        for tap in range(3):
            own_taps_ref[3 * which + tap : 3 * which + tap + 1, :] = both[tap : tap + 1]
    own_taps_ref[6:8, :] = jnp.zeros((2, lanes), jnp.float32)

    for start in range(0, length, rows):
        piece = kernel_ref[:, start : start + rows]
        both = jnp.concatenate([piece, pltpu.roll(piece, half_rows, 1)], axis=0)
        turned = jnp.transpose(both)[:half_rows]
        if start == 0:
            gain = skip_ref[...]
            gains = jnp.concatenate([gain, jnp.zeros_like(gain)], axis=1)
            row = lax.broadcasted_iota(jnp.int32, turned.shape, 0)
            turned = turned + jnp.where(row == 0, gains, 0.0)
        signal[start // inner, start % inner // rows] = turned

    def load(group, tile):
        return signal[:, group, tile * TILE : (tile + 1) * TILE, :].reshape(HALF * TILE, lanes)

    def enter_dots(value):
        top = value.astype(jnp.bfloat16)
        rest = (value - top.astype(jnp.float32)).astype(jnp.bfloat16)
        return table_dot(enter_ref, top) + dot(enter_ref[0], rest)

    def put(index, start, value):
        top = value.astype(jnp.bfloat16)
        high[index, start : start + TILE, :] = top
        low[index, start : start + TILE, :] = (value - top.astype(jnp.float32)).astype(jnp.bfloat16)

    for part in range(2):
        expand(wide_ref[part], enter_ref.at[part])
    enter_stage(load, enter_dots, turn_ref, per, half_rows, put)
    copies[5].wait()


def spectrum_kernel(high, low, mix_hbm, *refs):
    *spec_refs, mix_out_ref, mix_ref, sems = refs
    copies = [
        pltpu.make_async_copy(mix_hbm, mix_ref, sems.at[0]),
        pltpu.make_async_copy(mix_hbm.at[0], mix_out_ref, sems.at[1]),
    ]
    for copy in copies:
        copy.start()
    for copy in copies:
        copy.wait()
    inner = high.shape[1] // 2
    lanes = high.shape[2]
    count = lanes // 2
    length = inner * HALF
    for first in range(0, PAIRS, 2):
        group = range(first, min(first + 2, PAIRS))
        top = jnp.concatenate([high[index] for index in group], axis=1)
        rest = jnp.concatenate([low[index] for index in group], axis=1)
        spec = table_dot(mix_ref, top) + dot(mix_ref[0], rest)
        for at, index in enumerate(group):
            pair = spec[:, at * lanes : (at + 1) * lanes]
            left = lanes_of((inner, lanes)) < count
            for side in range(2):
                if 2 * index + side == BINS:
                    break
                for part in range(2):
                    here = pair[part * inner : (part + 1) * inner]
                    there = swap(here)
                    value = jnp.where(left, there, here) if side else jnp.where(left, here, there)
                    if part:
                        value = jnp.where(left, value, -value)
                    weight = (1.0 if 2 * index + side in (0, HALF) else 2.0) / (2 * length)
                    value = value * weight
                    which, place = divmod(2 * index + side, BIN_GROUP)
                    spec_refs[which][place, part * inner : (part + 1) * inner, :] = value


def mended_tiles(recv_ref, own_taps_ref, group, rows):
    blocks, per, _, lanes = recv_ref.shape
    count = lanes // 2
    taps = own_taps_ref[...]
    edge = recv_ref[:, group, rows : rows + EXTRA, :].astype(jnp.float32)
    blank = jnp.zeros((1, EXTRA, lanes), jnp.float32)
    if group > 0:
        before = recv_ref[:, group - 1, rows : rows + EXTRA, :].astype(jnp.float32)
    else:
        shifted = recv_ref[: blocks - 1, per - 1, rows : rows + EXTRA, :].astype(jnp.float32)
        before = jnp.concatenate([blank, shifted], axis=0)
    if group < per - 1:
        after = recv_ref[:, group + 1, rows : rows + EXTRA, :].astype(jnp.float32)
    else:
        shifted = recv_ref[1:, 0, rows : rows + EXTRA, :].astype(jnp.float32)
        after = jnp.concatenate([shifted, blank], axis=0)
    row = lax.broadcasted_iota(jnp.int32, (EXTRA, lanes), 0)
    lane = lax.broadcasted_iota(jnp.int32, (EXTRA, lanes), 1)
    first, last = [], []
    for block in range(blocks):
        top = recv_ref[block, group, :TILE, :].astype(jnp.float32)
        part = top[:EXTRA]
        near = before[block]
        mix_v = part + taps[2:3] * pltpu.roll(near, 6, 0)
        mix_v = mix_v + jnp.where(row == 0, taps[1:2] * pltpu.roll(near, 5, 0), 0.0)
        mix_q = edge[block] + taps[5:6] * pltpu.roll(near, 4, 0)
        mix_q = mix_q + jnp.where(row == 0, taps[4:5] * pltpu.roll(near, 3, 0), 0.0)
        fixed = jnp.where(part == jnp.inf, 0.0, mix_q * mix_v)
        fixed = jnp.where((row < 2) & (lane < count), fixed, part)
        first.append(jnp.concatenate([fixed, top[EXTRA:]], axis=0).astype(jnp.bfloat16))

        end = recv_ref[block, group, rows - TILE : rows, :].astype(jnp.float32)
        part = end[EXTRA:]
        near = after[block]
        mix_v = part + taps[2:3] * pltpu.roll(near, 4, 0)
        mix_v = mix_v + jnp.where(row == 7, taps[1:2] * pltpu.roll(near, 5, 0), 0.0)
        mix_q = pltpu.roll(edge[block], 6, 0) + taps[5:6] * pltpu.roll(near, 2, 0)
        mix_q = mix_q + jnp.where(row == 7, taps[4:5] * pltpu.roll(near, 3, 0), 0.0)
        fixed = jnp.where(part == jnp.inf, 0.0, mix_q * mix_v)
        fixed = jnp.where((row >= 6) & (lane >= count), fixed, part)
        last.append(jnp.concatenate([end[:EXTRA], fixed], axis=0).astype(jnp.bfloat16))
    return jnp.stack(first), jnp.stack(last)


def filter_kernel(recv_ref, own_taps_ref, core_ref, turn_ref, *refs):
    *spec_refs, mix_ref, out_ref, sections, returned, enter_ref, wide_ref = refs
    expand(core_ref[...], enter_ref)
    blocks, per, padded, lanes = recv_ref.shape
    rows = padded - EXTRA
    inner = per * rows
    tiles = rows // TILE

    def put(bin_index, start, real, imag):
        sections[bin_index, start : start + TILE, :] = real.astype(jnp.bfloat16)
        sections[bin_index, inner + start : inner + start + TILE, :] = imag.astype(jnp.bfloat16)

    for group in range(per):
        first, last = mended_tiles(recv_ref, own_taps_ref, group, rows)
        loaded = [first]
        for tile in range(1, tiles - 1):
            loaded.append(recv_ref[:, group, tile * TILE : (tile + 1) * TILE, :])
        loaded.append(last)
        loaded = [value.reshape(blocks * TILE, lanes) for value in loaded]
        def section_of(tile):
            return dot(enter_ref[...], jnp.concatenate(loaded[tile : tile + 2], axis=1))

        order = list(range(2, tiles - 2, 2)) + [0, tiles - 2]
        ahead = section_of(order[0])
        for place, tile in enumerate(order):
            section = ahead
            if place + 1 < len(order):
                ahead = section_of(order[place + 1])
            at = group * tiles + tile
            store_sections(section[:, :lanes], turn_ref, wide_ref, at, lanes, put)
            store_sections(section[:, lanes:], turn_ref, wide_ref, at + 1, lanes, put)

    def bins_from(first):
        return range(first, min(first + 2, BINS))

    def spec_of(first):
        pair = [sections[b] for b in bins_from(first)]
        return dot(mix_ref[...], jnp.concatenate(pair, axis=1))

    def back_of(first, spec):
        gains = [spec_refs[b // BIN_GROUP][b % BIN_GROUP] for b in bins_from(first)]
        gain = jnp.concatenate(gains, axis=1)
        real, imag = spec[:inner], spec[inner:]
        gain_real, gain_imag = gain[:inner], gain[inner:]
        product = jnp.concatenate(
            [real * gain_real - imag * gain_imag, -real * gain_imag - imag * gain_real], axis=0
        ).astype(jnp.bfloat16)
        return dot(mix_ref[...], product)

    def store_returned(first, back):
        for at, b in enumerate(bins_from(first)):
            real = back[:inner, at * lanes : (at + 1) * lanes]
            imag = back[inner:, at * lanes : (at + 1) * lanes]
            cos, sin = wide_ref[b, 0], wide_ref[b, 1]
            returned[slot(b, 0)] = (real * cos + imag * sin).astype(jnp.bfloat16)
            if b not in (0, HALF):
                returned[slot(b, 1)] = (real * sin - imag * cos).astype(jnp.bfloat16)

    ahead, behind = spec_of(0), None
    for first in range(0, BINS, 2):
        spec = ahead
        if first + 2 < BINS:
            ahead = spec_of(first + 2)
        back = back_of(first, spec)
        if behind is not None:
            store_returned(first - 2, behind)
        behind = back
    store_returned(BINS - 1, behind)

    leave = jnp.transpose(enter_ref[...])
    for tile in range(0, inner // TILE, 2):
        pair = jnp.concatenate(
            [
                returned[:, at * TILE : (at + 1) * TILE, :].reshape(OUTER * TILE, lanes)
                for at in (tile, tile + 1)
            ],
            axis=1,
        )
        value = dot(leave, pair).astype(jnp.bfloat16)
        group, place = divmod(tile, tiles)
        for at in (0, 1):
            start = (place + at) * TILE
            out_ref[:, group, start : start + TILE, :] = value[
                :, at * lanes : (at + 1) * lanes
            ].reshape(blocks, TILE, lanes)


def mixing_kernel(
    ret_ref, fwd_o_ref, rev_o_ref, fwd_ref, rev_ref, taps_ref, weight_ref, out_hbm,
    combined, total, out_ref, sems
):
    rows = fwd_ref.shape[0]
    width = weight_ref.shape[0]
    count = ret_ref.shape[2] // 2
    pieces = LANES // count
    blocks = width // LANES
    edge_row = lax.broadcasted_iota(jnp.int32, (EXTRA, LANES), 0)
    mirror = LANES - 1 - lax.broadcasted_iota(jnp.int32, (rows, LANES), 1)

    def near_edge(edges, block, target):
        low = block * LANES
        at_row = low // EDGE_LANES * EDGE_ROWS
        start = at_row // EXTRA * EXTRA
        at_lane = low % EDGE_LANES
        tile = edges[start : start + EXTRA, at_lane : at_lane + LANES]
        shift = (target - at_row + start) % EXTRA
        return pltpu.roll(tile, shift, 0) if shift else tile

    def columns(block):
        chunks = [ret_ref[block * pieces + piece].astype(jnp.float32) for piece in range(pieces)]
        if pieces == 2:
            return trade(*chunks)
        return [
            jnp.concatenate([c[:, which * count : (which + 1) * count] for c in chunks], axis=1)
            for which in range(2)
        ]

    def fwd_gate(block):
        low = 2 * width + block * LANES
        taps = taps_ref[:, low : low + LANES]
        mixed = short_filter(fwd_ref[:, low : low + LANES].astype(jnp.float32), taps, False)
        more = jnp.where(edge_row < 2, taps[2:3] * near_edge(fwd_o_ref, block, 0), 0.0)
        last = jnp.where(edge_row == 0, taps[1:2] * near_edge(fwd_o_ref, block, -1), 0.0)
        return jnp.concatenate([mixed[:EXTRA] + more + last, mixed[EXTRA:]], axis=0)

    def rev_gate(block):
        low = 2 * width + block * LANES
        taps = taps_ref[:, low : low + LANES]
        mixed = short_filter(rev_ref[:, low : low + LANES].astype(jnp.float32), taps, True)
        more = jnp.where(edge_row >= 6, taps[2:3] * near_edge(rev_o_ref, block, 6), 0.0)
        first = jnp.where(edge_row == 7, taps[1:2] * near_edge(rev_o_ref, block, 7), 0.0)
        tail = mixed[rows - EXTRA :] + more + first
        return jnp.concatenate([mixed[: rows - EXTRA], tail], axis=0)

    def product_of(start, end):
        part = slice(start * LANES, end * LANES)
        return dot(combined[:, part], weight_ref[part, :])

    half = blocks // 2
    for block in range(half):
        pair = (block, blocks - 1 - block)
        found = [columns(b) for b in pair]
        for at, b in enumerate(pair):
            gated = fwd_gate(b) * found[at][0]
            gate = rev_gate(pair[1 - at]) * found[1 - at][1]
            turned = jnp.take_along_axis(gate, mirror, axis=1)
            combined[:, b * LANES : (b + 1) * LANES] = (gated + turned).astype(jnp.bfloat16)
        if 2 * block + 2 == half:
            total[...] = product_of(0, block + 1) + product_of(blocks - 1 - block, blocks)
    middle = half // 2
    part = slice(middle * LANES, (blocks - middle) * LANES)
    copies = []
    for side in range(2):
        columns_out = pl.ds(side * (width // 2), width // 2)
        product = dot(combined[:, part], weight_ref[part, columns_out])
        out_ref[:, columns_out] = (total[:, columns_out] + product).astype(jnp.bfloat16)
        copy = pltpu.make_async_copy(
            out_ref.at[:, columns_out], out_hbm.at[:, columns_out], sems.at[side]
        )
        copy.start()
        copies.append(copy)
    for copy in copies:
        copy.wait()


HBM = pl.BlockSpec(memory_space=pltpu.HBM)
VMEM = pl.BlockSpec(memory_space=pltpu.VMEM)
SMEM = pl.BlockSpec(memory_space=pltpu.SMEM)


def params(limit=VMEM_BYTES):
    return pltpu.CompilerParams(vmem_limit_bytes=limit)


def cost(flops, size):
    return pl.CostEstimate(flops=flops, bytes_accessed=size, transcendentals=0)


def exchange(value):
    return lax.all_to_all(value, "ctx", split_axis=0, concat_axis=0, tiled=True)


def shifted(value, steps):
    count = lax.axis_size("ctx")
    first, end = max(0, -steps), min(count, count - steps)
    return lax.ppermute(value, "ctx", [(source, source + steps) for source in range(first, end)])


def per_device(fwd_proj, rev_proj, tokens, short_taps, long_kernel, skip_gain, out_weight):
    rows = fwd_proj.shape[0]
    half_rows = rows // 2
    width = fwd_proj.shape[1] // 3
    count, length = long_kernel.shape
    devices = length // rows
    lanes = 2 * count
    inner = length // HALF
    per = devices // HALF
    padded = rows + EXTRA
    edge_block = (EDGE_ROWS * width // EDGE_LANES, EDGE_LANES)
    tables = [jnp.asarray(table) for table in dft_tables(length)]
    core, mix, phases = tables
    outer_shape = (OUTER * TILE, HALF * TILE)
    block = (devices, padded, lanes)

    sent, fwd_o, rev_o = pl.pallas_call(
        gate_kernel,
        out_shape=(
            jax.ShapeDtypeStruct(block, jnp.bfloat16),
            jax.ShapeDtypeStruct(edge_block, jnp.float32),
            jax.ShapeDtypeStruct(edge_block, jnp.float32),
        ),
        in_specs=[HBM] * 4,
        out_specs=(HBM,) * 3,
        scratch_shapes=[
            pltpu.VMEM((rows, 2 * width), jnp.bfloat16),
            pltpu.VMEM((rows, 2 * width), jnp.bfloat16),
            pltpu.VMEM((TILE, width), jnp.bfloat16),
            pltpu.VMEM((TILE, width), jnp.bfloat16),
            pltpu.VMEM((1, rows), jnp.int32),
            pltpu.VMEM(short_taps.shape, jnp.float32),
            pltpu.VMEM(block, jnp.bfloat16),
            pltpu.VMEM(edge_block, jnp.float32),
            pltpu.VMEM(edge_block, jnp.float32),
            pltpu.VMEM((EXTRA, width), jnp.float32),
            pltpu.SemaphoreType.DMA((rows // CHUNK, 2)),
            pltpu.SemaphoreType.DMA((6,)),
            pltpu.SemaphoreType.DMA((rows // CHUNK,)),
        ],
        compiler_params=params(FULL_VMEM_BYTES),
        name="gate",
    )(fwd_proj, rev_proj, tokens.reshape(1, rows), short_taps)


    me = lax.axis_index("ctx").astype(jnp.int32).reshape(1)
    sent, me = lax.optimization_barrier((sent, me))
    received = exchange(sent)
    section_shape = jax.ShapeDtypeStruct((PAIRS, 2 * inner, lanes), jnp.bfloat16)
    spectrum_cost = cost(3 * PAIRS * 2 * (2 * inner) ** 2 * lanes, 4 * 1024 * 1024)
    high, low, own_taps, own_core, own_phases = pl.pallas_call(
        sections_kernel,
        out_shape=(
            section_shape,
            section_shape,
            jax.ShapeDtypeStruct((8, lanes), jnp.float32),
            jax.ShapeDtypeStruct(core.shape[1:], jnp.float32),
            jax.ShapeDtypeStruct(phases.shape, jnp.float32),
        ),
        in_specs=[SMEM] + [HBM] * 5,
        out_specs=(VMEM,) * 5,
        scratch_shapes=[
            pltpu.VMEM((count, length), jnp.float32),
            pltpu.VMEM((1, count), jnp.float32),
            pltpu.VMEM(short_taps.shape, jnp.float32),
            pltpu.VMEM(core.shape, jnp.float32),
            pltpu.VMEM((2,) + outer_shape, jnp.bfloat16),
            pltpu.VMEM((PAIRS, 2, inner, lanes), jnp.float32),
            pltpu.VMEM((HALF, per, half_rows, lanes), jnp.float32),
            pltpu.SemaphoreType.DMA((6,)),
        ],
        compiler_params=params(),
        cost_estimate=spectrum_cost,
        name="sections",
    )(me, long_kernel, skip_gain.reshape(1, count), short_taps, core, phases)

    own_taps, fwd_o, rev_o = lax.optimization_barrier((own_taps, fwd_o, rev_o))
    fwd_o = shifted(fwd_o, 1)
    rev_o = shifted(rev_o, -1)
    own_taps, fwd_o, rev_o = lax.optimization_barrier((own_taps, fwd_o, rev_o))

    groups = [min(BIN_GROUP, BINS - first) for first in range(0, BINS, BIN_GROUP)]
    spectrum = pl.pallas_call(
        spectrum_kernel,
        out_shape=tuple(
            jax.ShapeDtypeStruct((group, 2 * inner, lanes), jnp.float32) for group in groups
        )
        + (jax.ShapeDtypeStruct(mix.shape[1:], jnp.bfloat16),),
        in_specs=[VMEM, VMEM, HBM],
        out_specs=(VMEM,) * (len(groups) + 1),
        scratch_shapes=[
            pltpu.VMEM(mix.shape, jnp.bfloat16),
            pltpu.SemaphoreType.DMA((2,)),
        ],
        compiler_params=params(),
        cost_estimate=spectrum_cost,
        name="spectrum",
    )(high, low, mix)

    filtered = pl.pallas_call(
        filter_kernel,
        out_shape=jax.ShapeDtypeStruct((HALF, per, rows, lanes), jnp.bfloat16),
        in_specs=[VMEM] * (4 + len(spectrum)),
        out_specs=VMEM,
        scratch_shapes=[
            pltpu.VMEM((BINS, 2 * inner, lanes), jnp.bfloat16),
            pltpu.VMEM((OUTER, inner, lanes), jnp.bfloat16),
            pltpu.VMEM(outer_shape, jnp.bfloat16),
            pltpu.VMEM((BINS, 2, inner, lanes), jnp.float32),
        ],
        compiler_params=params(),
        cost_estimate=cost(4 * PAIRS * 4 * (2 * inner) ** 2 * lanes, 4 * 1024 * 1024),
        name="filter",
    )(received.reshape(HALF, per, padded, lanes), own_taps, own_core, own_phases, *spectrum)

    returned = exchange(filtered.reshape(devices, rows, lanes))

    return pl.pallas_call(
        mixing_kernel,
        out_shape=jax.ShapeDtypeStruct((rows, width), jnp.bfloat16),
        in_specs=[VMEM] * 7,
        out_specs=HBM,
        scratch_shapes=[
            pltpu.VMEM((rows, width), jnp.bfloat16),
            pltpu.VMEM((rows, width), jnp.float32),
            pltpu.VMEM((rows, width), jnp.bfloat16),
            pltpu.SemaphoreType.DMA((2,)),
        ],
        compiler_params=params(),
        cost_estimate=cost(2 * rows * width * width, 4 * 1024 * 1024),
        name="mixing",
    )(returned, fwd_o, rev_o, fwd_proj, rev_proj, short_taps, out_weight)


def solution(mesh):
    in_specs = (
        P(("dp", "ctx"), None),
        P(("dp", "ctx"), None),
        P(("dp", "ctx")),
        P(),
        P("ctx", None),
        P("ctx"),
        P(),
    )
    out_specs = P(("dp", "ctx"), None)
    return jax.shard_map(
        per_device, mesh=mesh, in_specs=in_specs, out_specs=out_specs, check_vma=False
    )
```

```python
import functools

import jax
import jax.numpy as jnp
import ml_dtypes
import numpy as np
from jax import lax
from jax.experimental import pallas as pl
from jax.experimental.pallas import tpu as pltpu
from jax.sharding import PartitionSpec as P

OUTER = 32
HALF = OUTER // 2
BINS = HALF + 1
PAIRS = (BINS + 1) // 2
EXTRA = 8
LANES = 128
TILE = 16
CHUNK = 64
BIN_GROUP = 2
VMEM_BYTES = 30 * 1024 * 1024
EDGE_LANES = 256
EDGE_ROWS = 2
FULL_VMEM_BYTES = 60000000


def split_table(table):
    high = table.astype(np.float32).astype(ml_dtypes.bfloat16)
    low = (table - high.astype(np.float64)).astype(np.float32).astype(ml_dtypes.bfloat16)
    return np.stack([high, low])


def outer_rows():
    rows = [(0, 0), (HALF, 0)]
    for bin_index in range(1, HALF):
        rows += [(bin_index, 0), (bin_index, 1)]
    return rows


def dft_tables(length):
    inner = length // HALF
    total = 2 * length
    blocks = np.arange(HALF)
    enter = np.zeros((OUTER, HALF))
    for row, (bin_index, part) in enumerate(outer_rows()):
        phase = 2.0 * np.pi * (bin_index * blocks % OUTER) / OUTER
        enter[row] = -np.sin(phase) if part else np.cos(phase)
    angles = 2.0 * np.pi * (np.outer(np.arange(inner), np.arange(inner)) % inner) / inner
    cos, sin = np.cos(angles), np.sin(angles)
    mix = np.block([[cos, sin], [-sin, cos]])
    turn = np.zeros((inner, LANES))
    turn_phase = 2.0 * np.pi * np.outer(np.arange(inner), np.arange(BINS)) / total
    turn[:, :BINS] = np.cos(turn_phase)
    turn[:, LANES // 2 : LANES // 2 + BINS] = np.sin(turn_phase)
    core = np.repeat(split_table(enter).astype(np.float32), TILE, axis=2)
    return (
        core,
        split_table(mix),
        turn.astype(np.float32),
    )


def dot(left, right):
    return jnp.dot(left, right, preferred_element_type=jnp.float32)


def table_dot(table_ref, right):
    return dot(table_ref[0], right) + dot(table_ref[1], right)


def lanes_of(shape):
    return lax.broadcasted_iota(jnp.int32, shape, len(shape) - 1)


def swap(value):
    lanes = value.shape[1]
    if lanes == LANES:
        return pltpu.roll(value, lanes // 2, 1)
    return jnp.concatenate([value[:, lanes // 2 :], value[:, : lanes // 2]], axis=1)


def trade(one, two):
    left = lanes_of(one.shape) < one.shape[1] // 2
    middle = swap(jnp.where(left, two, one))
    return jnp.where(left, one, middle), jnp.where(left, middle, two)


def left_halves(one, two):
    value = one if one is not None else two
    left = lanes_of(value.shape) < value.shape[1] // 2
    one = jnp.zeros_like(value) if one is None else one
    two = jnp.zeros_like(value) if two is None else swap(two)
    return jnp.where(left, one, two)


def right_halves(one, two):
    value = one if one is not None else two
    left = lanes_of(value.shape) < value.shape[1] // 2
    one = jnp.zeros_like(value) if one is None else swap(one)
    two = jnp.zeros_like(value) if two is None else two
    return jnp.where(left, one, two)


def slot(bin_index, part):
    if bin_index >= BINS or (part and bin_index in (0, HALF)):
        return None
    if bin_index in (0, HALF):
        return bin_index // HALF
    return 2 * bin_index + part


def enter_stage(load, dots, turn_ref, per, half_rows, put):
    inner = 2 * per * half_rows
    for group in range(per):
        for tile in range(0, half_rows // TILE, 2):
            pair = [load(group, tile), load(group, tile + 1)]
            lanes = pair[0].shape[1]
            section = dots(jnp.concatenate(pair, axis=1))
            for which in range(2):
                by_row = section[:, which * lanes : (which + 1) * lanes].reshape(OUTER, TILE, lanes)

                def part_of(bin_index, part):
                    row = slot(bin_index, part)
                    return None if row is None else by_row[row]

                for index in range(PAIRS):
                    bins = (2 * index, 2 * index + 1)
                    reals = [part_of(b, 0) for b in bins]
                    imags = [part_of(b, 1) for b in bins]
                    for side, halves in enumerate((left_halves, right_halves)):
                        start = (2 * group + side) * half_rows + (tile + which) * TILE
                        cos = turn_ref[index, 0, start : start + TILE, :]
                        sin = turn_ref[index, 1, start : start + TILE, :]
                        real = halves(*reals)
                        if imags[0] is None and imags[1] is None:
                            put(index, start, real * cos)
                            put(index, inner + start, real * -sin)
                        else:
                            imag = halves(*imags)
                            put(index, start, real * cos + imag * sin)
                            put(index, inner + start, imag * cos - real * sin)


def expand(core, target):
    row = lax.broadcasted_iota(jnp.int32, (TILE, core.shape[1]), 0)
    same = row == lanes_of(row.shape) % TILE
    for index in range(OUTER):
        wide = jnp.broadcast_to(core[index : index + 1], row.shape)
        target[index * TILE : (index + 1) * TILE, :] = jnp.where(same, wide, 0.0).astype(jnp.bfloat16)


def turn_pair(turn_ref, start, count, bin_index, lanes):
    rows = pl.ds(start, count)
    cos = jnp.broadcast_to(turn_ref[rows, bin_index : bin_index + 1], (count, lanes))
    at = LANES // 2 + bin_index
    sin = jnp.broadcast_to(turn_ref[rows, at : at + 1], (count, lanes))
    return cos, sin


def store_sections(section, turn_ref, wide_ref, tile, lanes, put):
    start = tile * TILE
    by_row = section.reshape(OUTER, TILE, lanes)
    for bin_index in range(BINS):
        cos, sin = turn_pair(turn_ref, start, TILE, bin_index, lanes)
        wide_ref[bin_index, 0, start : start + TILE, :] = cos
        wide_ref[bin_index, 1, start : start + TILE, :] = sin
        if bin_index in (0, HALF):
            real = by_row[0 if bin_index == 0 else 1]
            put(bin_index, start, real * cos, real * -sin)
        else:
            real = by_row[2 * bin_index]
            imag = by_row[2 * bin_index + 1]
            put(bin_index, start, real * cos + imag * sin, imag * cos - real * sin)


def short_filter(value, taps, later, near=None):
    rows = value.shape[0]
    row = lax.broadcasted_iota(jnp.int32, (EXTRA, LANES), 0)
    shifted = []
    for lag in (1, 2):
        moved = pltpu.roll(value, rows - lag if later else lag, 0)
        shift = EXTRA - lag if later else lag
        fill = 0.0 if near is None else pltpu.roll(near, shift, 0)
        if later:
            tail = jnp.where(row < EXTRA - lag, moved[rows - EXTRA :], fill)
            moved = jnp.concatenate([moved[: rows - EXTRA], tail], axis=0)
        else:
            head = jnp.where(row >= lag, moved[:EXTRA], fill)
            moved = jnp.concatenate([head, moved[EXTRA:]], axis=0)
        shifted.append(moved)
    return taps[0:1] * value + taps[1:2] * shifted[0] + taps[2:3] * shifted[1]


def chunk_filter(ref, start, columns, taps, later):
    end = start + CHUNK
    value = ref[start:end, columns].astype(jnp.float32)
    near = None
    if later and end < ref.shape[0]:
        near = ref[end : end + TILE, columns].astype(jnp.float32)[:EXTRA]
    elif not later and start > 0:
        near = ref[start - TILE : start, columns].astype(jnp.float32)[EXTRA:]
    return short_filter(value, taps, later, near)


def gate_kernel(
    fwd_hbm, rev_hbm, tokens_hbm, taps_hbm, out_hbm, fwd_o_hbm, rev_o_hbm,
    fwd_ref, rev_ref, fwd_edge_ref, rev_edge_ref, tokens_ref, taps_ref, out_ref, fwd_o_ref, rev_o_ref,
    first_q_ref, sems, small_sems, out_sems
):
    rows = fwd_ref.shape[0]
    width = fwd_ref.shape[1] // 2
    lanes = out_ref.shape[2]
    count = lanes // 2
    small = [
        pltpu.make_async_copy(taps_hbm, taps_ref, small_sems.at[0]),
        pltpu.make_async_copy(tokens_hbm, tokens_ref, small_sems.at[1]),
        pltpu.make_async_copy(
            fwd_hbm.at[pl.ds(rows - TILE, TILE), pl.ds(2 * width, width)],
            fwd_edge_ref,
            small_sems.at[2],
        ),
        pltpu.make_async_copy(
            rev_hbm.at[pl.ds(0, TILE), pl.ds(2 * width, width)], rev_edge_ref, small_sems.at[3]
        ),
    ]
    loads, stores = [], []
    for step in range(rows // CHUNK):
        start, end = step * CHUNK, (step + 1) * CHUNK
        rev_start = start + TILE if step else 0
        rev_end = min(end + TILE, rows)
        part = (pl.ds(start, CHUNK), pl.ds(0, 2 * width))
        rev_part = (pl.ds(rev_start, rev_end - rev_start), pl.ds(0, 2 * width))
        copies = [
            pltpu.make_async_copy(fwd_hbm.at[part], fwd_ref.at[part], sems.at[step, 0]),
            pltpu.make_async_copy(rev_hbm.at[rev_part], rev_ref.at[rev_part], sems.at[step, 1]),
        ]
        for copy in copies:
            copy.start()
        loads.append(copies)
        if step == 0:
            for copy in small[:2]:
                copy.start()
    for copy in small[2:]:
        copy.start()
    for copy in small[:2]:
        copy.wait()
    known_row = jnp.where(tokens_ref[...] != 4, 1.0, 0.0).astype(jnp.float32)
    known = jnp.transpose(jnp.broadcast_to(known_row, (LANES, rows)))
    edge_row = lax.broadcasted_iota(jnp.int32, (EXTRA, LANES), 0)

    def piece_of(left, right, piece):
        left_shift = (LANES - piece * count) % LANES
        right_shift = (LANES + count - piece * count) % LANES
        left = pltpu.roll(left, left_shift, 1) if left_shift else left
        right = pltpu.roll(right, right_shift, 1) if right_shift else right
        return jnp.where(lanes_of(left.shape) < count, left, right)[:, :lanes].astype(jnp.bfloat16)

    def pieces_of(left, right):
        if pieces != 2:
            return [piece_of(left, right, piece) for piece in range(pieces)]
        return [value.astype(jnp.bfloat16) for value in trade(left, right)]

    def rows_of(ref, columns, start):
        return ref[start : start + TILE, columns].astype(jnp.float32)

    def with_rows(edge, rows_at, value, at):
        moved = pltpu.roll(value, (rows_at - at) % EXTRA, 0)
        return jnp.where((edge_row >= rows_at) & (edge_row < rows_at + 2), moved, edge)

    pieces = LANES // count
    for step in range(rows // CHUNK):
        start = step * CHUNK
        final = start + CHUNK == rows
        for copy in loads[step] + (small[2:] if final else []):
            copy.wait()
        here = slice(start, start + CHUNK)
        for block in range(width // LANES):
            low = block * LANES
            at_v = slice(low, low + LANES)
            at_q = slice(width + low, width + low + LANES)
            taps_v, taps_q = taps_ref[:, at_v], taps_ref[:, at_q]
            fwd_v = chunk_filter(fwd_ref, start, at_v, taps_v, False)
            fwd_q = chunk_filter(fwd_ref, start, at_q, taps_q, False)
            fwd_body = known[here] * fwd_q * fwd_v
            rev_v = chunk_filter(rev_ref, start, at_v, taps_v, True)
            rev_q = chunk_filter(rev_ref, start, at_q, taps_q, True)
            rev_body = known[here] * rev_q * rev_v
            if start == 0:
                part = jnp.where(known[:EXTRA] > 0.0, fwd_v[:EXTRA], jnp.inf)
                head = jnp.where(edge_row < 2, part, fwd_body[:EXTRA])
                fwd_body = jnp.concatenate([head, fwd_body[EXTRA:]], axis=0)
                first_q_ref[:, at_v] = fwd_q[:EXTRA]
            if final:
                part = jnp.where(known[rows - EXTRA :] > 0.0, rev_v[CHUNK - EXTRA :], jnp.inf)
                tail = jnp.where(edge_row >= EXTRA - 2, part, rev_body[CHUNK - EXTRA :])
                rev_body = jnp.concatenate([rev_body[: CHUNK - EXTRA], tail], axis=0)
                raw_o = rows_of(fwd_edge_ref, at_v, 0)[EXTRA:]
                edge = jnp.where(edge_row < 2, first_q_ref[:, at_v], raw_o)
                edge = with_rows(edge, 2, rows_of(fwd_ref, at_v, rows - TILE)[EXTRA:], 6)
                edge = with_rows(edge, 4, rows_of(fwd_ref, at_q, rows - TILE)[EXTRA:], 6)
                fwd_body = jnp.concatenate([fwd_body, edge], axis=0)
                place = (
                    slice(low // EDGE_LANES * EDGE_ROWS, (low // EDGE_LANES + 1) * EDGE_ROWS),
                    slice(low % EDGE_LANES, low % EDGE_LANES + LANES),
                )
                fwd_o_ref[place] = pltpu.roll(raw_o, 2, 0)[:EDGE_ROWS]
                raw_o = rows_of(rev_edge_ref, at_v, 0)[:EXTRA]
                edge = jnp.where(edge_row < 2, pltpu.roll(rev_q[CHUNK - EXTRA :], 2, 0), 0.0)
                edge = with_rows(edge, 2, rows_of(rev_ref, at_v, 0)[:EXTRA], 0)
                edge = with_rows(edge, 4, rows_of(rev_ref, at_q, 0)[:EXTRA], 0)
                rev_body = jnp.concatenate([rev_body, edge], axis=0)
                rev_o_ref[place] = raw_o[:EDGE_ROWS]
            for piece, value in enumerate(pieces_of(fwd_body, rev_body)):
                out_ref[block * pieces + piece, start : start + value.shape[0], :] = value
            wide = width // LANES // 2
            if block % wide == wide - 1:
                part = (
                    pl.ds((block + 1 - wide) * pieces, wide * pieces),
                    pl.ds(start, CHUNK + (EXTRA if final else 0)),
                )
                copy = pltpu.make_async_copy(
                    out_ref.at[part], out_hbm.at[part], out_sems.at[step, block // wide]
                )
                copy.start()
                stores.append(copy)
    for at, (source, target) in enumerate(((fwd_o_ref, fwd_o_hbm), (rev_o_ref, rev_o_hbm))):
        copy = pltpu.make_async_copy(source, target, small_sems.at[4 + at])
        copy.start()
        stores.append(copy)
    for copy in stores:
        copy.wait()


def sections_kernel(
    me_ref, kernel_hbm, skip_hbm, taps_hbm, core_hbm, phase_hbm,
    high, low, own_taps_ref, core_ref, phase_ref,
    kernel_ref, skip_ref, taps_ref, wide_ref, enter_ref, turn_ref, signal, sems
):
    moves = (
        (phase_hbm, phase_ref), (kernel_hbm, kernel_ref), (skip_hbm, skip_ref),
        (taps_hbm, taps_ref), (core_hbm, wide_ref), (core_hbm.at[0], core_ref),
    )
    copies = [
        pltpu.make_async_copy(source, target, sems.at[at])
        for at, (source, target) in enumerate(moves)
    ]
    for copy in copies:
        copy.start()
    count, length = kernel_ref.shape
    lanes = 2 * count
    inner = length // HALF
    half_rows = signal.shape[2]
    rows = 2 * half_rows
    per = inner // rows
    width = taps_ref.shape[1] // 3

    copies[0].wait()
    for index in range(PAIRS):
        for part in range(2):
            columns = [part * (LANES // 2) + min(2 * index + b, BINS) for b in range(2)]
            sides = [
                jnp.broadcast_to(phase_ref[:, column : column + 1], (inner, lanes))
                for column in columns
            ]
            turn_ref[index, part] = jnp.where(lanes_of((inner, lanes)) < count, *sides)

    for copy in copies[1:5]:
        copy.wait()
    me = me_ref[0]
    per_block = LANES // count
    block = me // per_block
    shift = lax.rem(LANES - (me - block * per_block) * count, LANES)
    for which in range(2):
        column = pl.multiple_of(which * width + block * LANES, LANES)
        own = pltpu.roll(taps_ref[:, pl.ds(column, LANES)], shift, 1)
        both = jnp.where(lanes_of(own.shape) < count, own, pltpu.roll(own, count, 1))[:, :lanes]
        for tap in range(3):
            own_taps_ref[3 * which + tap : 3 * which + tap + 1, :] = both[tap : tap + 1]
    own_taps_ref[6:8, :] = jnp.zeros((2, lanes), jnp.float32)

    for start in range(0, length, rows):
        piece = kernel_ref[:, start : start + rows]
        both = jnp.concatenate([piece, pltpu.roll(piece, half_rows, 1)], axis=0)
        turned = jnp.transpose(both)[:half_rows]
        if start == 0:
            gain = skip_ref[...]
            gains = jnp.concatenate([gain, jnp.zeros_like(gain)], axis=1)
            row = lax.broadcasted_iota(jnp.int32, turned.shape, 0)
            turned = turned + jnp.where(row == 0, gains, 0.0)
        signal[start // inner, start % inner // rows] = turned

    def load(group, tile):
        return signal[:, group, tile * TILE : (tile + 1) * TILE, :].reshape(HALF * TILE, lanes)

    def enter_dots(value):
        top = value.astype(jnp.bfloat16)
        rest = (value - top.astype(jnp.float32)).astype(jnp.bfloat16)
        return table_dot(enter_ref, top) + dot(enter_ref[0], rest)

    def put(index, start, value):
        top = value.astype(jnp.bfloat16)
        high[index, start : start + TILE, :] = top
        low[index, start : start + TILE, :] = (value - top.astype(jnp.float32)).astype(jnp.bfloat16)

    for part in range(2):
        expand(wide_ref[part], enter_ref.at[part])
    enter_stage(load, enter_dots, turn_ref, per, half_rows, put)
    copies[5].wait()


def spectrum_kernel(high, low, mix_hbm, *refs):
    *spec_refs, mix_out_ref, mix_ref, sems = refs
    copies = [
        pltpu.make_async_copy(mix_hbm, mix_ref, sems.at[0]),
        pltpu.make_async_copy(mix_hbm.at[0], mix_out_ref, sems.at[1]),
    ]
    for copy in copies:
        copy.start()
    for copy in copies:
        copy.wait()
    inner = high.shape[1] // 2
    lanes = high.shape[2]
    count = lanes // 2
    length = inner * HALF
    for first in range(0, PAIRS, 2):
        group = range(first, min(first + 2, PAIRS))
        top = jnp.concatenate([high[index] for index in group], axis=1)
        rest = jnp.concatenate([low[index] for index in group], axis=1)
        spec = table_dot(mix_ref, top) + dot(mix_ref[0], rest)
        for at, index in enumerate(group):
            pair = spec[:, at * lanes : (at + 1) * lanes]
            left = lanes_of((inner, lanes)) < count
            for side in range(2):
                if 2 * index + side == BINS:
                    break
                for part in range(2):
                    here = pair[part * inner : (part + 1) * inner]
                    there = swap(here)
                    value = jnp.where(left, there, here) if side else jnp.where(left, here, there)
                    if part:
                        value = jnp.where(left, value, -value)
                    weight = (1.0 if 2 * index + side in (0, HALF) else 2.0) / (2 * length)
                    value = value * weight
                    which, place = divmod(2 * index + side, BIN_GROUP)
                    spec_refs[which][place, part * inner : (part + 1) * inner, :] = value


def mended_tiles(recv_ref, own_taps_ref, group, rows):
    blocks, per, _, lanes = recv_ref.shape
    count = lanes // 2
    taps = own_taps_ref[...]
    edge = recv_ref[:, group, rows : rows + EXTRA, :].astype(jnp.float32)
    blank = jnp.zeros((1, EXTRA, lanes), jnp.float32)
    if group > 0:
        before = recv_ref[:, group - 1, rows : rows + EXTRA, :].astype(jnp.float32)
    else:
        shifted = recv_ref[: blocks - 1, per - 1, rows : rows + EXTRA, :].astype(jnp.float32)
        before = jnp.concatenate([blank, shifted], axis=0)
    if group < per - 1:
        after = recv_ref[:, group + 1, rows : rows + EXTRA, :].astype(jnp.float32)
    else:
        shifted = recv_ref[1:, 0, rows : rows + EXTRA, :].astype(jnp.float32)
        after = jnp.concatenate([shifted, blank], axis=0)
    row = lax.broadcasted_iota(jnp.int32, (EXTRA, lanes), 0)
    lane = lax.broadcasted_iota(jnp.int32, (EXTRA, lanes), 1)
    first, last = [], []
    for block in range(blocks):
        top = recv_ref[block, group, :TILE, :].astype(jnp.float32)
        part = top[:EXTRA]
        near = before[block]
        mix_v = part + taps[2:3] * pltpu.roll(near, 6, 0)
        mix_v = mix_v + jnp.where(row == 0, taps[1:2] * pltpu.roll(near, 5, 0), 0.0)
        mix_q = edge[block] + taps[5:6] * pltpu.roll(near, 4, 0)
        mix_q = mix_q + jnp.where(row == 0, taps[4:5] * pltpu.roll(near, 3, 0), 0.0)
        fixed = jnp.where(part == jnp.inf, 0.0, mix_q * mix_v)
        fixed = jnp.where((row < 2) & (lane < count), fixed, part)
        first.append(jnp.concatenate([fixed, top[EXTRA:]], axis=0).astype(jnp.bfloat16))

        end = recv_ref[block, group, rows - TILE : rows, :].astype(jnp.float32)
        part = end[EXTRA:]
        near = after[block]
        mix_v = part + taps[2:3] * pltpu.roll(near, 4, 0)
        mix_v = mix_v + jnp.where(row == 7, taps[1:2] * pltpu.roll(near, 5, 0), 0.0)
        mix_q = pltpu.roll(edge[block], 6, 0) + taps[5:6] * pltpu.roll(near, 2, 0)
        mix_q = mix_q + jnp.where(row == 7, taps[4:5] * pltpu.roll(near, 3, 0), 0.0)
        fixed = jnp.where(part == jnp.inf, 0.0, mix_q * mix_v)
        fixed = jnp.where((row >= 6) & (lane >= count), fixed, part)
        last.append(jnp.concatenate([end[:EXTRA], fixed], axis=0).astype(jnp.bfloat16))
    return jnp.stack(first), jnp.stack(last)


def filter_kernel(recv_ref, own_taps_ref, core_ref, turn_ref, *refs):
    *spec_refs, mix_ref, out_ref, sections, returned, enter_ref, wide_ref = refs
    expand(core_ref[...], enter_ref)
    blocks, per, padded, lanes = recv_ref.shape
    rows = padded - EXTRA
    inner = per * rows
    tiles = rows // TILE

    def put(bin_index, start, real, imag):
        sections[bin_index, start : start + TILE, :] = real.astype(jnp.bfloat16)
        sections[bin_index, inner + start : inner + start + TILE, :] = imag.astype(jnp.bfloat16)

    for group in range(per):
        first, last = mended_tiles(recv_ref, own_taps_ref, group, rows)
        loaded = [first]
        for tile in range(1, tiles - 1):
            loaded.append(recv_ref[:, group, tile * TILE : (tile + 1) * TILE, :])
        loaded.append(last)
        loaded = [value.reshape(blocks * TILE, lanes) for value in loaded]
        def section_of(tile):
            return dot(enter_ref[...], jnp.concatenate(loaded[tile : tile + 2], axis=1))

        order = list(range(2, tiles - 2, 2)) + [0, tiles - 2]
        ahead = section_of(order[0])
        for place, tile in enumerate(order):
            section = ahead
            if place + 1 < len(order):
                ahead = section_of(order[place + 1])
            at = group * tiles + tile
            store_sections(section[:, :lanes], turn_ref, wide_ref, at, lanes, put)
            store_sections(section[:, lanes:], turn_ref, wide_ref, at + 1, lanes, put)

    def bins_from(first):
        return range(first, min(first + 2, BINS))

    def spec_of(first):
        pair = [sections[b] for b in bins_from(first)]
        return dot(mix_ref[...], jnp.concatenate(pair, axis=1))

    def back_of(first, spec):
        gains = [spec_refs[b // BIN_GROUP][b % BIN_GROUP] for b in bins_from(first)]
        gain = jnp.concatenate(gains, axis=1)
        real, imag = spec[:inner], spec[inner:]
        gain_real, gain_imag = gain[:inner], gain[inner:]
        product = jnp.concatenate(
            [real * gain_real - imag * gain_imag, -real * gain_imag - imag * gain_real], axis=0
        ).astype(jnp.bfloat16)
        return dot(mix_ref[...], product)

    def store_returned(first, back):
        for at, b in enumerate(bins_from(first)):
            real = back[:inner, at * lanes : (at + 1) * lanes]
            imag = back[inner:, at * lanes : (at + 1) * lanes]
            cos, sin = wide_ref[b, 0], wide_ref[b, 1]
            returned[slot(b, 0)] = (real * cos + imag * sin).astype(jnp.bfloat16)
            if b not in (0, HALF):
                returned[slot(b, 1)] = (real * sin - imag * cos).astype(jnp.bfloat16)

    ahead, behind = spec_of(0), None
    for first in range(0, BINS, 2):
        spec = ahead
        if first + 2 < BINS:
            ahead = spec_of(first + 2)
        back = back_of(first, spec)
        if behind is not None:
            store_returned(first - 2, behind)
        behind = back
    store_returned(BINS - 1, behind)

    leave = jnp.transpose(enter_ref[...])
    for tile in range(0, inner // TILE, 2):
        pair = jnp.concatenate(
            [
                returned[:, at * TILE : (at + 1) * TILE, :].reshape(OUTER * TILE, lanes)
                for at in (tile, tile + 1)
            ],
            axis=1,
        )
        value = dot(leave, pair).astype(jnp.bfloat16)
        group, place = divmod(tile, tiles)
        for at in (0, 1):
            start = (place + at) * TILE
            out_ref[:, group, start : start + TILE, :] = value[
                :, at * lanes : (at + 1) * lanes
            ].reshape(blocks, TILE, lanes)


def mixing_kernel(
    ret_ref, fwd_o_ref, rev_o_ref, fwd_ref, rev_ref, taps_ref, weight_ref, out_hbm,
    combined, total, out_ref, sems
):
    rows = fwd_ref.shape[0]
    width = weight_ref.shape[0]
    count = ret_ref.shape[2] // 2
    pieces = LANES // count
    blocks = width // LANES
    edge_row = lax.broadcasted_iota(jnp.int32, (EXTRA, LANES), 0)
    mirror = LANES - 1 - lax.broadcasted_iota(jnp.int32, (rows, LANES), 1)

    def near_edge(edges, block, target):
        low = block * LANES
        at_row = low // EDGE_LANES * EDGE_ROWS
        start = at_row // EXTRA * EXTRA
        at_lane = low % EDGE_LANES
        tile = edges[start : start + EXTRA, at_lane : at_lane + LANES]
        shift = (target - at_row + start) % EXTRA
        return pltpu.roll(tile, shift, 0) if shift else tile

    def columns(block):
        chunks = [ret_ref[block * pieces + piece].astype(jnp.float32) for piece in range(pieces)]
        if pieces == 2:
            return trade(*chunks)
        return [
            jnp.concatenate([c[:, which * count : (which + 1) * count] for c in chunks], axis=1)
            for which in range(2)
        ]

    def fwd_gate(block):
        low = 2 * width + block * LANES
        taps = taps_ref[:, low : low + LANES]
        mixed = short_filter(fwd_ref[:, low : low + LANES].astype(jnp.float32), taps, False)
        more = jnp.where(edge_row < 2, taps[2:3] * near_edge(fwd_o_ref, block, 0), 0.0)
        last = jnp.where(edge_row == 0, taps[1:2] * near_edge(fwd_o_ref, block, -1), 0.0)
        return jnp.concatenate([mixed[:EXTRA] + more + last, mixed[EXTRA:]], axis=0)

    def rev_gate(block):
        low = 2 * width + block * LANES
        taps = taps_ref[:, low : low + LANES]
        mixed = short_filter(rev_ref[:, low : low + LANES].astype(jnp.float32), taps, True)
        more = jnp.where(edge_row >= 6, taps[2:3] * near_edge(rev_o_ref, block, 6), 0.0)
        first = jnp.where(edge_row == 7, taps[1:2] * near_edge(rev_o_ref, block, 7), 0.0)
        tail = mixed[rows - EXTRA :] + more + first
        return jnp.concatenate([mixed[: rows - EXTRA], tail], axis=0)

    def product_of(start, end):
        part = slice(start * LANES, end * LANES)
        return dot(combined[:, part], weight_ref[part, :])

    half = blocks // 2
    for block in range(half):
        pair = (block, blocks - 1 - block)
        found = [columns(b) for b in pair]
        for at, b in enumerate(pair):
            gated = fwd_gate(b) * found[at][0]
            gate = rev_gate(pair[1 - at]) * found[1 - at][1]
            turned = jnp.take_along_axis(gate, mirror, axis=1)
            combined[:, b * LANES : (b + 1) * LANES] = (gated + turned).astype(jnp.bfloat16)
        if 2 * block + 2 == half:
            total[...] = product_of(0, block + 1) + product_of(blocks - 1 - block, blocks)
    middle = half // 2
    part = slice(middle * LANES, (blocks - middle) * LANES)
    copies = []
    for side in range(2):
        columns_out = pl.ds(side * (width // 2), width // 2)
        product = dot(combined[:, part], weight_ref[part, columns_out])
        out_ref[:, columns_out] = (total[:, columns_out] + product).astype(jnp.bfloat16)
        copy = pltpu.make_async_copy(
            out_ref.at[:, columns_out], out_hbm.at[:, columns_out], sems.at[side]
        )
        copy.start()
        copies.append(copy)
    for copy in copies:
        copy.wait()


HBM = pl.BlockSpec(memory_space=pltpu.HBM)
VMEM = pl.BlockSpec(memory_space=pltpu.VMEM)
SMEM = pl.BlockSpec(memory_space=pltpu.SMEM)


def params(limit=VMEM_BYTES):
    return pltpu.CompilerParams(vmem_limit_bytes=limit)


def cost(flops, size):
    return pl.CostEstimate(flops=flops, bytes_accessed=size, transcendentals=0)


def exchange(value):
    return lax.all_to_all(value, "ctx", split_axis=0, concat_axis=0, tiled=True)


def shifted(value, steps):
    count = lax.axis_size("ctx")
    first, end = max(0, -steps), min(count, count - steps)
    return lax.ppermute(value, "ctx", [(source, source + steps) for source in range(first, end)])


def per_device(fwd_proj, rev_proj, tokens, short_taps, long_kernel, skip_gain, out_weight):
    rows = fwd_proj.shape[0]
    half_rows = rows // 2
    width = fwd_proj.shape[1] // 3
    count, length = long_kernel.shape
    devices = length // rows
    lanes = 2 * count
    inner = length // HALF
    per = devices // HALF
    padded = rows + EXTRA
    edge_block = (EDGE_ROWS * width // EDGE_LANES, EDGE_LANES)
    tables = [jnp.asarray(table) for table in dft_tables(length)]
    core, mix, phases = tables
    outer_shape = (OUTER * TILE, HALF * TILE)
    block = (devices, padded, lanes)

    sent, fwd_o, rev_o = pl.pallas_call(
        gate_kernel,
        out_shape=(
            jax.ShapeDtypeStruct(block, jnp.bfloat16),
            jax.ShapeDtypeStruct(edge_block, jnp.float32),
            jax.ShapeDtypeStruct(edge_block, jnp.float32),
        ),
        in_specs=[HBM] * 4,
        out_specs=(HBM,) * 3,
        scratch_shapes=[
            pltpu.VMEM((rows, 2 * width), jnp.bfloat16),
            pltpu.VMEM((rows, 2 * width), jnp.bfloat16),
            pltpu.VMEM((TILE, width), jnp.bfloat16),
            pltpu.VMEM((TILE, width), jnp.bfloat16),
            pltpu.VMEM((1, rows), jnp.int32),
            pltpu.VMEM(short_taps.shape, jnp.float32),
            pltpu.VMEM(block, jnp.bfloat16),
            pltpu.VMEM(edge_block, jnp.float32),
            pltpu.VMEM(edge_block, jnp.float32),
            pltpu.VMEM((EXTRA, width), jnp.float32),
            pltpu.SemaphoreType.DMA((rows // CHUNK, 2)),
            pltpu.SemaphoreType.DMA((6,)),
            pltpu.SemaphoreType.DMA((rows // CHUNK, 2)),
        ],
        compiler_params=params(FULL_VMEM_BYTES),
        name="gate",
    )(fwd_proj, rev_proj, tokens.reshape(1, rows), short_taps)


    me = lax.axis_index("ctx").astype(jnp.int32).reshape(1)
    sent, me = lax.optimization_barrier((sent, me))
    received = exchange(sent)
    section_shape = jax.ShapeDtypeStruct((PAIRS, 2 * inner, lanes), jnp.bfloat16)
    spectrum_cost = cost(3 * PAIRS * 2 * (2 * inner) ** 2 * lanes, 4 * 1024 * 1024)
    high, low, own_taps, own_core, own_phases = pl.pallas_call(
        sections_kernel,
        out_shape=(
            section_shape,
            section_shape,
            jax.ShapeDtypeStruct((8, lanes), jnp.float32),
            jax.ShapeDtypeStruct(core.shape[1:], jnp.float32),
            jax.ShapeDtypeStruct(phases.shape, jnp.float32),
        ),
        in_specs=[SMEM] + [HBM] * 5,
        out_specs=(VMEM,) * 5,
        scratch_shapes=[
            pltpu.VMEM((count, length), jnp.float32),
            pltpu.VMEM((1, count), jnp.float32),
            pltpu.VMEM(short_taps.shape, jnp.float32),
            pltpu.VMEM(core.shape, jnp.float32),
            pltpu.VMEM((2,) + outer_shape, jnp.bfloat16),
            pltpu.VMEM((PAIRS, 2, inner, lanes), jnp.float32),
            pltpu.VMEM((HALF, per, half_rows, lanes), jnp.float32),
            pltpu.SemaphoreType.DMA((6,)),
        ],
        compiler_params=params(),
        cost_estimate=spectrum_cost,
        name="sections",
    )(me, long_kernel, skip_gain.reshape(1, count), short_taps, core, phases)

    own_taps, fwd_o, rev_o = lax.optimization_barrier((own_taps, fwd_o, rev_o))
    fwd_o = shifted(fwd_o, 1)
    rev_o = shifted(rev_o, -1)
    own_taps, fwd_o, rev_o = lax.optimization_barrier((own_taps, fwd_o, rev_o))

    groups = [min(BIN_GROUP, BINS - first) for first in range(0, BINS, BIN_GROUP)]
    spectrum = pl.pallas_call(
        spectrum_kernel,
        out_shape=tuple(
            jax.ShapeDtypeStruct((group, 2 * inner, lanes), jnp.float32) for group in groups
        )
        + (jax.ShapeDtypeStruct(mix.shape[1:], jnp.bfloat16),),
        in_specs=[VMEM, VMEM, HBM],
        out_specs=(VMEM,) * (len(groups) + 1),
        scratch_shapes=[
            pltpu.VMEM(mix.shape, jnp.bfloat16),
            pltpu.SemaphoreType.DMA((2,)),
        ],
        compiler_params=params(),
        cost_estimate=spectrum_cost,
        name="spectrum",
    )(high, low, mix)

    filtered = pl.pallas_call(
        filter_kernel,
        out_shape=jax.ShapeDtypeStruct((HALF, per, rows, lanes), jnp.bfloat16),
        in_specs=[VMEM] * (4 + len(spectrum)),
        out_specs=VMEM,
        scratch_shapes=[
            pltpu.VMEM((BINS, 2 * inner, lanes), jnp.bfloat16),
            pltpu.VMEM((OUTER, inner, lanes), jnp.bfloat16),
            pltpu.VMEM(outer_shape, jnp.bfloat16),
            pltpu.VMEM((BINS, 2, inner, lanes), jnp.float32),
        ],
        compiler_params=params(),
        cost_estimate=cost(4 * PAIRS * 4 * (2 * inner) ** 2 * lanes, 4 * 1024 * 1024),
        name="filter",
    )(received.reshape(HALF, per, padded, lanes), own_taps, own_core, own_phases, *spectrum)

    returned = exchange(filtered.reshape(devices, rows, lanes))

    return pl.pallas_call(
        mixing_kernel,
        out_shape=jax.ShapeDtypeStruct((rows, width), jnp.bfloat16),
        in_specs=[VMEM] * 7,
        out_specs=HBM,
        scratch_shapes=[
            pltpu.VMEM((rows, width), jnp.bfloat16),
            pltpu.VMEM((rows, width), jnp.float32),
            pltpu.VMEM((rows, width), jnp.bfloat16),
            pltpu.SemaphoreType.DMA((2,)),
        ],
        compiler_params=params(),
        cost_estimate=cost(2 * rows * width * width, 4 * 1024 * 1024),
        name="mixing",
    )(returned, fwd_o, rev_o, fwd_proj, rev_proj, short_taps, out_weight)


def solution(mesh):
    in_specs = (
        P(("dp", "ctx"), None),
        P(("dp", "ctx"), None),
        P(("dp", "ctx")),
        P(),
        P("ctx", None),
        P("ctx"),
        P(),
    )
    out_specs = P(("dp", "ctx"), None)
    return jax.shard_map(
        per_device, mesh=mesh, in_specs=in_specs, out_specs=out_specs, check_vma=False
    )
```
